128 devices in a mesh: dp: 8 (over x, y_lo), seq: 16 (over z, y_hi, core).
Axes of the slice: x: 4, y: 4 (y_hi: 2, y_lo: 2; y = y_hi * 2 + y_lo), z: 4, core: 2. Of those that a mesh axis runs over, the one named last changes fastest.
Arguments:
- section_input: bfloat16 [65536, 1536], P(('dp', 'seq')), parts along dimension 0, may hold values from -6 to 6
- conv_gain: float32 [1536], replicated, may hold values from 0.1 to 1.9
- conv_weight: bfloat16 [5, 1536, 1536], replicated, may hold values from -0.0625 to 0.0625
- conv_bias: float32 [1536], replicated, may hold values from -3 to 3
- attn_gain: float32 [1536], replicated, may hold values from 0.1 to 1.9
- q_weight: bfloat16 [1536, 1024], P('seq'), may hold values from -5 to 5
- kv_weight: bfloat16 [1536, 320], P('seq'), may hold values from -0.15625 to 0.15625
- o_weight: bfloat16 [1536, 1536], P('seq'), may hold values from -0.15625 to 0.15625
Outputs:
- skip: bfloat16 [32768, 1536], P(('dp', 'seq')), parts along dimension 0
- block_out: bfloat16 [32768, 1536], P(('dp', 'seq')), parts along dimension 0
The draws below stay inside these ranges and needn't reach their ends.
There are 8 independent parts, one for each index of `dp`. The reference program is written for one: setup_inputs(seed, part) draws one part's arguments, and reference() takes and returns one part's arrays. A program takes and returns all parts, laid end to end along the dimension named above; an argument that names none is the same for every part. Nothing has to cross between parts.
All inputs are finite; a program needn't handle non-finite values.
Results may differ from the reference program's by a relative error of at most 0.008.
The reference program's roundings to bfloat16 on the way count: a program that leaves them out, or rounds other values in their place, can miss the bound.
Values may be sent and summed in bfloat16 or wider, within the bound.
No kernel may reach another device: no remote copies, remote signals or barrier semaphores. Data moves between devices by JAX's collectives and lax.ppermute only.
A program may use at most 192 MiB of HBM per device.

```python
import jax
import jax.numpy as jnp
from jax import lax

D = 1536
HEADS = 8
DK = 128
DV = 192
TAPS = 5
TOKENS = 4096
POSITIONS = 8192
HV = 1536


def draw_q_weight(key, part):
    scale_key = jax.random.fold_in(key, 11)
    entry_key = jax.random.fold_in(key, 12)
    lower, upper = (1.0, 4.0)
    head_scales = jnp.exp(jax.random.uniform(scale_key, (HEADS,), jnp.float32, jnp.log(lower), jnp.log(upper)))
    entries = jax.random.truncated_normal(entry_key, -4.0, 4.0, (D, HEADS * DK), jnp.float32)
    column_scales = jnp.repeat(head_scales, DK) / jnp.sqrt(jnp.float32(D))
    return (entries * column_scales[None, :]).astype(jnp.bfloat16)


def levels(key, dims, pieces, low, high):
    level = 1.0
    for position, blocks in pieces:
        steps = jax.random.uniform(jax.random.fold_in(jax.random.fold_in(key, 6), position), (blocks,), jnp.float32, low / len(pieces), high / len(pieces))
        level = level * jnp.repeat(jnp.exp(steps), dims[position] // blocks).reshape((-1,) + (1,) * (len(dims) - 1 - position))
    return level


def bell_draw(stream_key, shape, spread, most, pieces=(), kind=jnp.bfloat16):
    result = jax.random.normal(stream_key, shape, jnp.float32) * spread
    if len(pieces) > 0:
        result = levels(stream_key, shape, pieces, -0.22, 0.18) * result
    return jnp.clip(result, min=-most, max=most).astype(kind)


def setup_inputs(seed: int = 0, part: int = 0) -> dict:
    seeds = jax.random.split(jax.random.key(seed), 9)
    part_keys = jax.random.split(jax.random.fold_in(seeds[8], part), 9)
    return {
        "section_input": bell_draw(part_keys[0], (POSITIONS, D), 1.0, 6.0, ((0, 16),)),
        "conv_gain": jnp.clip(1.0 + 0.18 * jax.random.normal(seeds[1], (D,), jnp.float32), 0.1, 1.9),
        "conv_weight": bell_draw(seeds[2], (TAPS, D, D), (TAPS * D) ** -0.5, 0.0625),
        "conv_bias": bell_draw(seeds[3], (D,), 0.5, 3.0, (), jnp.float32),
        "attn_gain": jnp.clip(1.0 + 0.18 * jax.random.normal(seeds[4], (D,), jnp.float32), 0.1, 1.9),
        "q_weight": draw_q_weight(jax.random.fold_in(seeds[8], 71), part),
        "kv_weight": bell_draw(seeds[6], (D, DK + DV), D ** -0.5, 0.15625, ((0, 16),)),
        "o_weight": bell_draw(seeds[7], (HV, D), HV ** -0.5, 0.15625, ((0, 16),)),
    }


def rms_scale(rows, gain):
    values = rows.astype(jnp.float32)
    return values * lax.rsqrt(lax.optimization_barrier(jnp.mean(values * values, axis=-1, keepdims=True)) + 1e-06) * gain

def rotate(values, positions):
    half_size = values.shape[-1] // 2
    freqs = jnp.power(10000.0, -jnp.arange(half_size, dtype=jnp.float32) / half_size)
    angle = positions.astype(jnp.float32)[:, None] * freqs[None, :]
    if values.ndim == 3:
        angle = angle[:, None, :]
    cosine = jnp.cos(angle)
    sine = jnp.sin(angle)
    first = values[..., :half_size]
    second = values[..., half_size:]
    return jnp.concatenate([first * cosine - second * sine, second * cosine + first * sine], axis=-1)

def reference(section_input, conv_gain, conv_weight, conv_bias, attn_gain, q_weight, kv_weight, o_weight):
    activated = jax.nn.gelu(rms_scale(section_input, conv_gain), approximate=True).astype(jnp.bfloat16)
    reach = TAPS // 2
    padded = jnp.pad(activated, ((reach, reach), (0, 0)))
    conv = jnp.zeros((POSITIONS, D), jnp.float32) + conv_bias
    for kernel_tap in range(TAPS):
        conv = conv + jnp.dot(padded[kernel_tap:kernel_tap + POSITIONS], conv_weight[kernel_tap], preferred_element_type=jnp.float32)
    summed = section_input.astype(jnp.float32) + conv
    skip = lax.optimization_barrier(jnp.max(summed.reshape(TOKENS, 2, D), axis=1)).astype(jnp.bfloat16)
    normed = rms_scale(skip, attn_gain).astype(jnp.bfloat16)
    positions = jnp.arange(TOKENS, dtype=jnp.int32)
    queries = jnp.dot(normed, q_weight, preferred_element_type=jnp.float32).reshape(TOKENS, HEADS, DK)
    queries = rotate(queries, positions).astype(jnp.bfloat16)
    projected = jnp.dot(normed, kv_weight, preferred_element_type=jnp.float32)
    keys = rotate(projected[:, :DK], positions).astype(jnp.bfloat16)
    values = projected[:, DK:].astype(jnp.bfloat16)
    score_scale = DK ** (-0.5)

    def one_head(head_queries):
        scores = jnp.dot(head_queries, keys.T, preferred_element_type=jnp.float32) * score_scale
        peak = lax.optimization_barrier(jnp.max(scores, axis=-1, keepdims=True))
        weights = jnp.exp(scores - peak)
        total = lax.optimization_barrier(jnp.sum(weights, axis=-1, keepdims=True))
        return jnp.dot(weights.astype(jnp.bfloat16), values, preferred_element_type=jnp.float32) / total
    heads_out = lax.map(one_head, jnp.transpose(queries, (1, 0, 2)))
    mixed = jnp.transpose(heads_out, (1, 0, 2)).reshape(TOKENS, HV).astype(jnp.bfloat16)
    attended = jnp.dot(mixed, o_weight, preferred_element_type=jnp.float32)
    block_out = (skip.astype(jnp.float32) + attended).astype(jnp.bfloat16)
    return (skip, block_out)
```

```python
import functools
import math

import jax
import jax.numpy as jnp
from jax import lax
from jax.experimental import pallas as pl
from jax.experimental.pallas import tpu as pltpu
from jax.sharding import PartitionSpec as P

HEADS = 8
DK = 128
DV = 192
EPS = 1e-06
BF = jnp.bfloat16
F32 = jnp.float32
AXES = ("dp", "seq")
VMEM_LIMIT = 60 * 1024 * 1024


def place(l):
    dp, s = divmod(l, 16)
    return dp // 2, dp % 2, s // 4, (s // 2) % 2, s % 2


def device(x, yl, z, yh, c):
    return ((x % 4) * 2 + yl) * 16 + (z % 4) * 4 + yh * 2 + c


def moves(f):
    return [(l, device(*f(*place(l)))) for l in range(128)]


def along_z(k):
    return moves(lambda x, yl, z, yh, c: (x, yl, z + k, yh, c))


def along_x(k):
    return moves(lambda x, yl, z, yh, c: (x + k, yl, z, yh, c))


OTHER_Y = moves(lambda x, yl, z, yh, c: (x, yl, z, 1 - yh, c))
NEAR_Y = moves(lambda x, yl, z, yh, c: (x, 1 - yl, z, 1 - yh, c))
OTHER_CORE = moves(lambda x, yl, z, yh, c: (x, yl, z, yh, 1 - c))


def send(array, pairs):
    return lax.ppermute(array, AXES, pairs)


def full(shape):
    return pl.BlockSpec(shape, lambda *_: (0,) * len(shape))


def gelu(v):
    return jax.nn.gelu(v, approximate=True)


def activate_kernel(x_ref, gain_ref, act_ref, raw_ref, act_s, raw_s):
    groups, rows, lanes = act_s.shape

    def step(i, _):
        at = pl.multiple_of(i * rows, rows)
        half = pl.ds(pl.multiple_of(i * (rows // 2), rows // 2), rows // 2)
        v = x_ref[pl.ds(at, rows), :].astype(F32)
        scale = lax.rsqrt(jnp.mean(v * v, axis=-1, keepdims=True) + EPS)
        g = gelu(v * scale * gain_ref[...])
        for k in range(groups):
            cols = slice(k * lanes, (k + 1) * lanes)
            raw_s[k] = v[:, cols]
            act_s[k] = g[:, cols]
            for j in range(2):
                act_ref[j, half, cols] = act_s[k, pl.ds(j, rows // 2, 2), :].astype(BF)
                raw_ref[j, half, cols] = raw_s[k, pl.ds(j, rows // 2, 2), :].astype(BF)
        return 0

    lax.fori_loop(0, x_ref.shape[0] // rows, step, 0)


def activate(x, gain):
    rows, width = x.shape
    out = jax.ShapeDtypeStruct((2, rows // 2, width), BF)
    return pl.pallas_call(
        activate_kernel,
        out_shape=(out, out),
        scratch_shapes=[pltpu.VMEM((width // 128, 64, 128), F32)] * 2,
        compiler_params=pltpu.CompilerParams(vmem_limit_bytes=VMEM_LIMIT),
        name="activate",
    )(x, gain[None])


def conv_kernel(
    taps, act_ref, raw_ref, before_ref, after_ref, cg_ref, b_ref, ag_ref, w_ref,
    skip_ref, norm_ref, lhs, wide,
):
    n = pl.program_id(0)
    rows, width = skip_ref.shape
    tile = w_ref.shape[2]

    @pl.when(n == 0)
    def _():
        def halo(ref):
            v = ref[...].astype(F32)
            return gelu(v * lax.rsqrt(jnp.mean(v * v, axis=-1, keepdims=True) + EPS) * cg_ref[...])

        before, after = halo(before_ref), halo(after_ref)
        for j in range(2):
            lhs[2 + j] = act_ref[j]
            wide[pl.ds(8, rows), :] = act_ref[j].astype(F32)
            wide[7:8, :] = before[j : j + 1]
            wide[rows + 8 : rows + 9, :] = after[j : j + 1]
            lhs[j] = wide[pl.ds(7, rows), :].astype(BF)
            lhs[4 + j] = wide[pl.ds(9, rows), :].astype(BF)

    acc = jnp.zeros((2 * rows, tile), F32)
    for t in range(taps):
        acc = acc + jnp.dot(
            lhs[t : t + 2].reshape(2 * rows, width), w_ref[t], preferred_element_type=F32
        )
    cols = pl.ds(pl.multiple_of(n * tile, tile), tile)
    bias = b_ref[:, cols]
    even = raw_ref[0, :, cols].astype(F32) + (acc[:rows] + bias)
    odd = raw_ref[1, :, cols].astype(F32) + (acc[rows:] + bias)
    skip_ref[:, cols] = jnp.maximum(even, odd).astype(BF)

    @pl.when(n == pl.num_programs(0) - 1)
    def _():
        v = skip_ref[...].astype(F32)
        scale = lax.rsqrt(jnp.mean(v * v, axis=-1, keepdims=True) + EPS)
        norm_ref[...] = (v * scale * ag_ref[...]).astype(BF)


def convolve(act, raw, before, after, conv_gain, conv_weight, conv_bias, attn_gain):
    _, rows, width = act.shape
    taps = conv_weight.shape[0]
    tile = 256
    out = jax.ShapeDtypeStruct((rows, width), BF)
    return pl.pallas_call(
        functools.partial(conv_kernel, taps),
        out_shape=(out, out),
        grid=(width // tile,),
        in_specs=[
            full((2, rows, width)),
            full((2, rows, width)),
            full((2, width)),
            full((2, width)),
            full((1, width)),
            full((1, width)),
            full((1, width)),
            pl.BlockSpec((taps, width, tile), lambda n: (0, 0, n)),
        ],
        out_specs=(full((rows, width)), full((rows, width))),
        scratch_shapes=[
            pltpu.VMEM((6, rows, width), BF),
            pltpu.VMEM((rows + 16, width), F32),
        ],
        compiler_params=pltpu.CompilerParams(vmem_limit_bytes=VMEM_LIMIT),
        name="conv",
    )(act, raw, before, after, conv_gain[None], conv_bias[None], attn_gain[None], conv_weight)


def gather_weight(shard, yh):
    other = send(shard, NEAR_Y)
    pair = jnp.where(
        yh == 0, jnp.concatenate([shard, other], 0), jnp.concatenate([other, shard], 0)
    )
    pieces = [pair, send(pair, along_z(1)), send(pair, along_z(-1)), send(pair, along_z(2))]
    return pieces + [send(p, OTHER_CORE) for p in pieces]


STEPS = (0, -1, 1, 2)


def weight_copies(where_ref, pieces, buf, sems):
    out = []
    each = pieces[0].shape[0] // 2
    for i, piece in enumerate(pieces):
        z = lax.rem(where_ref[0] + STEPS[i % 4] + 4, 4)
        core = where_ref[1] if i < 4 else 1 - where_ref[1]
        for yh in range(2):
            row = pl.multiple_of((z * 4 + yh * 2 + core) * each, each)
            out.append(
                pltpu.make_async_copy(
                    piece.at[pl.ds(yh * each, each), :],
                    buf.at[pl.ds(row, each), :],
                    sems.at[2 * i + yh],
                )
            )
    return out


def rotated(v, c, s):
    return v * c + pltpu.roll(v, DK // 2, 1) * s


def project_kernel(where_ref, norm_ref, cos_ref, sin_ref, *rest):
    pieces, (q_ref, kv_ref, buf, sems) = rest[:8], rest[8:]
    copies = weight_copies(where_ref, pieces, buf, sems)
    for c in copies:
        c.start()
    for c in copies:
        c.wait()
    x = norm_ref[...]
    rows = x.shape[0]
    kv = jnp.dot(x, buf[:, HEADS * DK :], preferred_element_type=F32)
    c, s = cos_ref[...], sin_ref[...]
    kv_ref[pl.ds(0, rows), :] = rotated(kv[:, :DK], c, s).astype(BF)
    kv_ref[pl.ds(rows, rows), :] = kv[:, DK : 2 * DK].astype(BF)
    tail = kv[:, 2 * DK :]
    kv_ref[pl.ds(2 * rows, rows // 2), :] = jnp.concatenate(
        [tail[: rows // 2], tail[rows // 2 :]], axis=1
    ).astype(BF)
    for h in range(HEADS):
        q = jnp.dot(x, buf[:, h * DK : (h + 1) * DK], preferred_element_type=F32)
        q_ref[h] = rotated(q, c, s).astype(BF)


def project(where, normed, cosine, sine, pieces):
    rows, width = normed.shape
    cols = pieces[0].shape[1]
    vm = pl.BlockSpec(memory_space=pltpu.VMEM)
    return pl.pallas_call(
        project_kernel,
        out_shape=(
            jax.ShapeDtypeStruct((HEADS, rows, DK), BF),
            jax.ShapeDtypeStruct((rows * 5 // 2, DK), BF),
        ),
        in_specs=[pl.BlockSpec(memory_space=pltpu.SMEM), vm, vm, vm]
        + [pl.BlockSpec(memory_space=pl.ANY)] * 8,
        scratch_shapes=[pltpu.VMEM((width, cols), BF), pltpu.SemaphoreType.DMA((16,))],
        compiler_params=pltpu.CompilerParams(vmem_limit_bytes=VMEM_LIMIT),
        name="project",
    )(where, normed, cosine, sine, *pieces)


def attention_kernel(counts, q_ref, *rest):
    parts = rest[: len(counts)]
    out_ref, kbuf, vbuf, tails, scores, peak, acc, sems = rest[len(counts) :]
    rows = q_ref.shape[1]
    copies = []
    p = 0
    for part, count in zip(parts, counts):
        for i in range(count):
            to = pl.ds(p * rows, rows)
            for j, (lo, size, dst) in enumerate(
                (
                    (0, rows, kbuf.at[to, :]),
                    (rows, rows, vbuf.at[to, pl.ds(0, DK)]),
                    (2 * rows, rows // 2, tails.at[p]),
                )
            ):
                copies.append(
                    pltpu.make_async_copy(part.at[i, pl.ds(lo, size), :], dst, sems.at[p, j])
                )
            p += 1
    for c in copies:
        c.start()
    for c in copies:
        c.wait()
    half = rows // 2
    lane = lax.broadcasted_iota(jnp.int32, (half, DK), 1)
    rest_lanes = jnp.where(lane == DK // 2, 1.0, 0.0)

    def unpack(i, _):
        t = tails[i].astype(F32)
        at = pl.multiple_of(i * rows, rows)
        vbuf[pl.ds(at, half), DK:] = jnp.where(lane < DK // 2, t, rest_lanes).astype(BF)
        vbuf[pl.ds(at + half, half), DK:] = jnp.where(
            lane < DK // 2, pltpu.roll(t, DK // 2, 1), rest_lanes
        ).astype(BF)
        return 0

    lax.fori_loop(0, p, unpack, 0)

    tokens = p * rows
    chunk = 512
    chunks = tokens // chunk
    per = 2
    block = per * rows
    scale = DK ** (-0.5) * math.log2(math.e)

    def keys_of(kc):
        return pl.ds(pl.multiple_of(kc * chunk, chunk), chunk)

    def make_scores(tile, kc, top):
        q = q_ref[pl.ds(tile * per, per)].reshape(block, DK)
        s = lax.dot_general(
            q, kbuf[keys_of(kc), :], (((1,), (1,)), ((), ())), preferred_element_type=F32
        )
        scores[tile % 2, kc] = s
        for j in range(chunk // DK):
            top = jnp.maximum(top, s[:, j * DK : (j + 1) * DK])
        return top

    def use_scores(tile, kc):
        m = peak[...]
        s = scores[tile % 2, kc]
        w = jnp.concatenate(
            [jnp.exp2((s[:, j * DK : (j + 1) * DK] - m) * scale) for j in range(chunk // DK)],
            axis=1,
        ).astype(BF)
        acc[...] += jnp.dot(w, vbuf[keys_of(kc), :], preferred_element_type=F32)

    def spread(top):
        peak[...] = jnp.broadcast_to(jnp.max(top, axis=-1, keepdims=True), (block, DK))

    lowest = jnp.full((block, DK), -jnp.inf, F32)
    tiles = HEADS // per
    spread(lax.fori_loop(0, chunks, lambda kc, top: make_scores(0, kc, top), lowest))
    for tile in range(tiles):
        acc[...] = jnp.zeros_like(acc)
        if tile + 1 < tiles:

            def both(kc, top, tile=tile):
                top = make_scores(tile + 1, kc, top)
                use_scores(tile, kc)
                return top

            top = lax.fori_loop(0, chunks, both, lowest)
        else:

            def last(kc, _, tile=tile):
                use_scores(tile, kc)
                return 0

            lax.fori_loop(0, chunks, last, 0)
        a = acc[...]
        o = a[:, :DV] / a[:, DV : DV + 1]
        out_ref[:, tile * per * DV : (tile + 1) * per * DV] = jnp.concatenate(
            [o[:rows], o[rows:]], axis=1
        ).astype(BF)
        if tile + 1 < tiles:
            spread(top)


def attention(q, parts):
    heads, rows, _ = q.shape
    counts = tuple(p.shape[0] for p in parts)
    total = sum(counts)
    tokens = total * rows
    vm = pl.BlockSpec(memory_space=pltpu.VMEM)
    return pl.pallas_call(
        functools.partial(attention_kernel, counts),
        out_shape=jax.ShapeDtypeStruct((rows, heads * DV), BF),
        in_specs=[vm] + [pl.BlockSpec(memory_space=pl.ANY)] * len(parts),
        scratch_shapes=[
            pltpu.VMEM((tokens, DK), BF),
            pltpu.VMEM((tokens, 2 * DK), BF),
            pltpu.VMEM((total, rows // 2, DK), BF),
            pltpu.VMEM((2, tokens // 512, 2 * rows, 512), F32),
            pltpu.VMEM((2 * rows, DK), F32),
            pltpu.VMEM((2 * rows, 2 * DK), F32),
            pltpu.SemaphoreType.DMA((total, 3)),
        ],
        compiler_params=pltpu.CompilerParams(vmem_limit_bytes=VMEM_LIMIT),
        name="attention",
    )(q, *parts)


def output_kernel(where_ref, mixed_ref, skip_ref, *rest):
    pieces, (out_ref, buf, sems) = rest[:8], rest[8:]
    copies = weight_copies(where_ref, pieces, buf, sems)
    for c in copies:
        c.start()
    for c in copies:
        c.wait()
    tile = 512
    for n in range(out_ref.shape[1] // tile):
        cols = slice(n * tile, (n + 1) * tile)
        y = jnp.dot(mixed_ref[...], buf[:, cols], preferred_element_type=F32)
        out_ref[:, cols] = (skip_ref[:, cols].astype(F32) + y).astype(BF)


def output(where, mixed, skip, pieces):
    rows, width = skip.shape
    vm = pl.BlockSpec(memory_space=pltpu.VMEM)
    return pl.pallas_call(
        output_kernel,
        out_shape=jax.ShapeDtypeStruct((rows, width), BF),
        in_specs=[pl.BlockSpec(memory_space=pltpu.SMEM), vm, vm]
        + [pl.BlockSpec(memory_space=pl.ANY)] * 8,
        scratch_shapes=[pltpu.VMEM((mixed.shape[1], width), BF), pltpu.SemaphoreType.DMA((16,))],
        compiler_params=pltpu.CompilerParams(vmem_limit_bytes=VMEM_LIMIT),
        name="output",
    )(where, mixed, skip, *pieces)


def gather_kv(own):
    own = own[None]
    pair = jnp.concatenate([own, send(own, OTHER_Y)], 0)
    parts = [pair, send(pair, along_z(1)), send(pair, along_z(-1)), send(pair, along_z(2))]
    return parts + [send(p, OTHER_CORE) for p in parts]


def rotation(seq, rows):
    half = DK // 2
    freqs = jnp.power(10000.0, -jnp.arange(half, dtype=F32) / half)
    positions = seq * rows + jnp.arange(rows, dtype=jnp.int32)
    angle = positions.astype(F32)[:, None] * freqs[None, :]
    c, s = jnp.cos(angle), jnp.sin(angle)
    return jnp.concatenate([c, c], 1), jnp.concatenate([-s, s], 1)


def body(x, conv_gain, conv_weight, conv_bias, attn_gain, q_weight, kv_weight, o_weight):
    rows = x.shape[0] // 2
    seq = lax.axis_index("seq")
    where = jnp.stack([seq // 4, seq % 2]).astype(jnp.int32)
    yh = (seq // 2) % 2
    count = lax.axis_size("seq")
    up = [(i, i + 1) for i in range(count - 1)]
    down = [(j, i) for i, j in up]
    before = lax.ppermute(x[-2:], "seq", up)
    after = lax.ppermute(x[:2], "seq", down)
    qkv_pieces = gather_weight(jnp.concatenate([q_weight, kv_weight], 1), yh)
    o_pieces = gather_weight(o_weight, yh)
    act, raw = activate(x, conv_gain)
    cosine, sine = rotation(seq, rows)
    skip, normed = convolve(
        act, raw, before, after, conv_gain, conv_weight, conv_bias, attn_gain
    )
    q, kv = project(where, normed, cosine, sine, qkv_pieces)
    mixed = attention(q, gather_kv(kv))
    return skip, output(where, mixed, skip, o_pieces)


def solution(mesh):
    rows = P(("dp", "seq"), None)
    in_specs = (rows, P(), P(), P(), P(), P("seq", None), P("seq", None), P("seq", None))
    return jax.shard_map(
        body, mesh=mesh, in_specs=in_specs, out_specs=(rows, rows), check_vma=False
    )
```

```python
import functools
import math

import jax
import jax.numpy as jnp
from jax import lax
from jax.experimental import pallas as pl
from jax.experimental.pallas import tpu as pltpu
from jax.sharding import PartitionSpec as P

HEADS = 8
DK = 128
DV = 192
EPS = 1e-06
BF = jnp.bfloat16
F32 = jnp.float32
AXES = ("dp", "seq")
VMEM_LIMIT = 60 * 1024 * 1024


def place(l):
    dp, s = divmod(l, 16)
    return dp // 2, dp % 2, s // 4, (s // 2) % 2, s % 2


def device(x, yl, z, yh, c):
    return ((x % 4) * 2 + yl) * 16 + (z % 4) * 4 + yh * 2 + c


def moves(f):
    return [(l, device(*f(*place(l)))) for l in range(128)]


def along_x(k):
    return moves(lambda x, yl, z, yh, c: (x + k, yl, z, yh, c))


OTHER_CORE = moves(lambda x, yl, z, yh, c: (x, yl, z, yh, 1 - c))


def send(array, pairs):
    return lax.ppermute(array, AXES, pairs)


def full(shape):
    return pl.BlockSpec(shape, lambda *_: (0,) * len(shape))


ANYWHERE = pl.BlockSpec(memory_space=pl.ANY)
IN_VMEM = pl.BlockSpec(memory_space=pltpu.VMEM)


def conv_kernel(
    x_ref, before_ref, after_ref, cg_ref, bias_ref, ag_ref, w_hbm,
    skip_ref, norm_ref, lhs, raw, wide, act_s, raw_s, w_buf, sems,
):
    n = pl.program_id(0)
    steps = pl.num_programs(0)
    rows, width = skip_ref.shape
    taps, _, tile = w_buf.shape[1:]

    def weights(i):
        cols = pl.ds(pl.multiple_of(i * tile, tile), tile)
        slot = lax.rem(i, 2)
        return pltpu.make_async_copy(w_hbm.at[:, :, cols], w_buf.at[slot], sems.at[slot])

    def activated(v):
        scale = lax.rsqrt(jnp.mean(v * v, axis=-1, keepdims=True) + EPS)
        return jax.nn.gelu(v * scale * cg_ref[...], approximate=True)

    @pl.when(n == 0)
    def _():
        weights(0).start()
        groups, some, lanes = act_s.shape

        def step(i, _):
            at = pl.multiple_of(i * some, some)
            half = pl.ds(pl.multiple_of(i * (some // 2), some // 2), some // 2)
            there = pl.ds(pl.multiple_of(i * (some // 2) + 8, 8), some // 2)
            v = x_ref[pl.ds(at, some), :].astype(F32)
            g = activated(v)
            for k in range(groups):
                cols = slice(k * lanes, (k + 1) * lanes)
                raw_s[k] = v[:, cols]
                act_s[k] = g[:, cols]
                for j in range(2):
                    a = act_s[k, pl.ds(j, some // 2, 2), :]
                    wide[j, there, cols] = a
                    lhs[2 + j, half, cols] = a.astype(BF)
                    raw[j, half, cols] = raw_s[k, pl.ds(j, some // 2, 2), :].astype(BF)
            return 0

        lax.fori_loop(0, x_ref.shape[0] // some, step, 0)
        before = activated(before_ref[...].astype(F32))
        after = activated(after_ref[...].astype(F32))
        for j in range(2):
            wide[j, 7:8, :] = before[j : j + 1]
            wide[j, rows + 8 : rows + 9, :] = after[j : j + 1]
            lhs[j] = wide[j, pl.ds(7, rows), :].astype(BF)
            lhs[4 + j] = wide[j, pl.ds(9, rows), :].astype(BF)

    @pl.when(n + 1 < steps)
    def _():
        weights(n + 1).start()

    weights(n).wait()
    slot = lax.rem(n, 2)
    acc = jnp.zeros((2 * rows, tile), F32)
    for t in range(taps):
        acc = acc + jnp.dot(
            lhs[t : t + 2].reshape(2 * rows, width), w_buf[slot, t], preferred_element_type=F32
        )
    cols = pl.ds(pl.multiple_of(n * tile, tile), tile)
    bias = bias_ref[:, cols]
    even = raw[0, :, cols].astype(F32) + (acc[:rows] + bias)
    odd = raw[1, :, cols].astype(F32) + (acc[rows:] + bias)
    skip_ref[:, cols] = jnp.maximum(even, odd).astype(BF)

    @pl.when(n == steps - 1)
    def _():
        v = skip_ref[...].astype(F32)
        scale = lax.rsqrt(jnp.mean(v * v, axis=-1, keepdims=True) + EPS)
        norm_ref[...] = (v * scale * ag_ref[...]).astype(BF)


def convolve(x, before, after, conv_gain, conv_weight, conv_bias, attn_gain):
    rows, width = x.shape[0] // 2, x.shape[1]
    taps = conv_weight.shape[0]
    tile = 256
    out = jax.ShapeDtypeStruct((rows, width), BF)
    vector = full((1, width))
    return pl.pallas_call(
        conv_kernel,
        out_shape=(out, out),
        grid=(width // tile,),
        in_specs=[full(x.shape), full((2, width)), full((2, width)), vector, vector, vector, ANYWHERE],
        out_specs=(full((rows, width)), full((rows, width))),
        scratch_shapes=[
            pltpu.VMEM((6, rows, width), BF),
            pltpu.VMEM((2, rows, width), BF),
            pltpu.VMEM((2, rows + 16, width), F32),
            pltpu.VMEM((width // 128, 128, 128), F32),
            pltpu.VMEM((width // 128, 128, 128), F32),
            pltpu.VMEM((2, taps, width, tile), BF),
            pltpu.SemaphoreType.DMA((2,)),
        ],
        compiler_params=pltpu.CompilerParams(vmem_limit_bytes=VMEM_LIMIT),
        name="conv",
    )(x, before, after, conv_gain[None], conv_bias[None], attn_gain[None], conv_weight)


def to_same_core(block):
    groups = [[i * 2 + c for i in range(8)] for c in range(2)]
    return lax.all_to_all(block, "seq", 0, 0, tiled=True, axis_index_groups=groups)


def swapped(pieces):
    return [send(p, OTHER_CORE) for p in pieces]


def own_place():
    return lax.axis_index("dp") // 2, lax.rem(lax.axis_index("seq"), 2)


def rows_of_halves(buf, core):
    p = lax.rem(own_place()[0], 2)
    return buf.at[p, :, core], buf.at[1 - p, pl.ds(0, 4), core], buf.at[1 - p, pl.ds(4, 4), core]


def rows_of_quarters(buf, core):
    x = own_place()[0]
    return tuple(buf.at[lax.rem(x + d, 4), :, core] for d in (0, 3, 1, 2))


def fill(rows_of, mine, theirs, buf, sems):
    c = own_place()[1]
    copies = []
    for core, pieces in ((c, mine), (1 - c, theirs)):
        for src, dst in zip(pieces, rows_of(buf, core)):
            copies.append(pltpu.make_async_copy(src, dst, sems.at[len(copies)]))
    for copy in copies:
        copy.start()
    return copies


def pack_kernel(q_hbm, o_hbm, kv_hbm, out_hbm, buf, in_sems, out_sems):
    x, _ = own_place()
    copies, at = [], 0
    for src, index, n in (
        (q_hbm, lax.rem(x, 2), q_hbm.shape[1] // 2),
        (o_hbm, x, o_hbm.shape[1] // 4),
        (kv_hbm, 0, kv_hbm.shape[1]),
    ):
        part = src.at[:, pl.ds(pl.multiple_of(index * n, 128), n)] if src is not kv_hbm else src
        copies.append(
            pltpu.make_async_copy(part, buf.at[:, pl.ds(at, n)], in_sems.at[len(copies)])
        )
        at += n
    for copy in copies:
        copy.start()
    for copy in copies:
        copy.wait()
    copies = [
        pltpu.make_async_copy(buf, out_hbm.at[i], out_sems.at[i]) for i in range(out_hbm.shape[0])
    ]
    for copy in copies:
        copy.start()
    for copy in copies:
        copy.wait()


def pack(q_weight, o_weight, kv_weight):
    rows = q_weight.shape[0]
    n = q_weight.shape[1] // 2 + o_weight.shape[1] // 4 + kv_weight.shape[1]
    return pl.pallas_call(
        pack_kernel,
        out_shape=jax.ShapeDtypeStruct((8, rows, n), BF),
        in_specs=[ANYWHERE] * 3,
        out_specs=ANYWHERE,
        scratch_shapes=[
            pltpu.VMEM((rows, n), BF),
            pltpu.SemaphoreType.DMA((3,)),
            pltpu.SemaphoreType.DMA((8,)),
        ],
        compiler_params=pltpu.CompilerParams(vmem_limit_bytes=VMEM_LIMIT),
        name="pack",
    )(q_weight, o_weight, kv_weight)


def rotated(v, c, s):
    return v * c + pltpu.roll(v, DK // 2, 1) * s


def kv_kernel(norm_ref, cos_ref, sin_ref, own, other, kv_ref, buf, sems):
    _, c = own_place()
    copies = [
        pltpu.make_async_copy(
            own.at[:, :, pl.ds(own.shape[2] - other.shape[2], other.shape[2])],
            buf.at[:, c],
            sems.at[0],
        ),
        pltpu.make_async_copy(other, buf.at[:, 1 - c], sems.at[1]),
    ]
    for copy in copies:
        copy.start()
    for copy in copies:
        copy.wait()
    x = norm_ref[...]
    rows, width = x.shape
    kv = jnp.dot(x, buf[...].reshape(width, buf.shape[-1]), preferred_element_type=F32)
    tail = kv[:, 2 * DK :]
    packed = jnp.concatenate(
        [
            rotated(kv[:, :DK], cos_ref[...], sin_ref[...]),
            kv[:, DK : 2 * DK],
            jnp.concatenate([tail[: rows // 2], tail[rows // 2 :]], axis=1),
        ],
        axis=0,
    ).astype(BF)
    for i in range(kv_ref.shape[0]):
        kv_ref[i] = packed


def key_values(normed, cosine, sine, own, other):
    rows = normed.shape[0]
    return pl.pallas_call(
        kv_kernel,
        out_shape=jax.ShapeDtypeStruct((8, rows * 5 // 2, DK), BF),
        in_specs=[IN_VMEM, IN_VMEM, IN_VMEM, ANYWHERE, ANYWHERE],
        scratch_shapes=[
            pltpu.VMEM((8, 2, *other.shape[1:]), BF),
            pltpu.SemaphoreType.DMA((2,)),
        ],
        compiler_params=pltpu.CompilerParams(vmem_limit_bytes=VMEM_LIMIT),
        name="key_values",
    )(normed, cosine, sine, own, other)


def query_kernel(norm_ref, cos_ref, sin_ref, *rest):
    gathered, *pieces = rest[:6]
    q_ref, buf, sems = rest[6:]
    mine = [gathered.at[:, :, pl.ds(0, buf.shape[-1])], *pieces[:2]]
    for copy in fill(rows_of_halves, mine, pieces[2:], buf, sems):
        copy.wait()
    x = norm_ref[...]
    width = x.shape[1]
    c, s = cos_ref[...], sin_ref[...]
    per = buf.shape[-1] // DK
    for p in range(2):
        y = jnp.dot(x, buf[p].reshape(width, per * DK), preferred_element_type=F32)
        for h in range(per):
            q_ref[p * per + h] = rotated(y[:, h * DK : (h + 1) * DK], c, s).astype(BF)


def queries(normed, cosine, sine, pieces):
    rows, _ = normed.shape
    return pl.pallas_call(
        query_kernel,
        out_shape=jax.ShapeDtypeStruct((HEADS, rows, DK), BF),
        in_specs=[IN_VMEM, IN_VMEM, IN_VMEM] + [ANYWHERE] * 6,
        scratch_shapes=[
            pltpu.VMEM((2, 8, 2, *pieces[1].shape[1:]), BF),
            pltpu.SemaphoreType.DMA((6,)),
        ],
        compiler_params=pltpu.CompilerParams(vmem_limit_bytes=VMEM_LIMIT),
        name="queries",
    )(normed, cosine, sine, *pieces)


def attention_kernel(
    q_ref, own, other, out_ref, kbuf, vbuf, tails, even_s, odd_s, peak, heads_s, sems
):
    heads, rows, _ = q_ref.shape
    slabs = kbuf.shape[0]
    half = rows // 2
    copies = []
    for i, part in enumerate((own, other)):
        to = pl.ds(i * (slabs // 2), slabs // 2)
        for lo, size, dst in (
            (0, rows, kbuf.at[to]),
            (rows, rows, vbuf.at[to, :, pl.ds(0, DK)]),
            (2 * rows, half, tails.at[to]),
        ):
            copies.append(
                pltpu.make_async_copy(part.at[:, pl.ds(lo, size), :], dst, sems.at[len(copies)])
            )
    for copy in copies:
        copy.start()
    for copy in copies:
        copy.wait()
    lane = lax.broadcasted_iota(jnp.int32, (half, DK), 1)
    ones = jnp.where(lane == DK // 2, 1.0, 0.0)
    for i in range(slabs):
        t = tails[i].astype(F32)
        vbuf[i, :half, DK:] = jnp.where(lane < DK // 2, t, ones).astype(BF)
        vbuf[i, half:, DK:] = jnp.where(
            lane < DK // 2, pltpu.roll(t, DK // 2, 1), ones
        ).astype(BF)

    chunks, _, chunk = even_s.shape
    n = chunk // rows
    scale = DK ** (-0.5) * math.log2(math.e)
    lowest = jnp.full((rows, DK), -jnp.inf, F32)

    def make_scores(head, to):
        top = lowest
        for kc in range(chunks):
            k = kbuf[kc * n : (kc + 1) * n].reshape(chunk, DK)
            s = lax.dot_general(
                q_ref[head], k, (((1,), (1,)), ((), ())), preferred_element_type=F32
            )
            to[kc] = s
            for j in range(chunk // DK):
                top = jnp.maximum(top, s[:, j * DK : (j + 1) * DK])
        return jnp.broadcast_to(jnp.max(top, axis=-1, keepdims=True), (rows, DK))

    def use_scores(head, scores, m):
        total = jnp.zeros((rows, 2 * DK), F32)
        for kc in range(chunks):
            s = scores[kc]
            w = jnp.concatenate(
                [jnp.exp2((s[:, j * DK : (j + 1) * DK] - m) * scale) for j in range(chunk // DK)],
                axis=1,
            ).astype(BF)
            v = vbuf[kc * n : (kc + 1) * n].reshape(chunk, 2 * DK)
            total = total + jnp.dot(w, v, preferred_element_type=F32)
        heads_s[head] = total[:, :DV] / total[:, DV : DV + 1]

    peak[...] = make_scores(0, even_s)

    def step(i, _):
        head = 2 * i
        m = peak[...]
        above = make_scores(head + 1, odd_s)
        use_scores(head, even_s, m)
        peak[...] = make_scores(head + 2, even_s)
        use_scores(head + 1, odd_s, above)
        return 0

    lax.fori_loop(0, heads // 2 - 1, step, 0)
    m = peak[...]
    above = make_scores(heads - 1, odd_s)
    use_scores(heads - 2, even_s, m)
    use_scores(heads - 1, odd_s, above)
    for h in range(0, heads, 2):
        out_ref[:, h * DV : (h + 2) * DV] = jnp.concatenate(
            [heads_s[h], heads_s[h + 1]], axis=1
        ).astype(BF)


def attention(q, own, other):
    heads, rows, _ = q.shape
    slabs = 2 * own.shape[0]
    tokens = slabs * rows
    chunk = 2048
    return pl.pallas_call(
        attention_kernel,
        out_shape=jax.ShapeDtypeStruct((rows, heads * DV), BF),
        in_specs=[IN_VMEM, ANYWHERE, ANYWHERE],
        scratch_shapes=[
            pltpu.VMEM((slabs, rows, DK), BF),
            pltpu.VMEM((slabs, rows, 2 * DK), BF),
            pltpu.VMEM((slabs, rows // 2, DK), BF),
            pltpu.VMEM((tokens // chunk, rows, chunk), F32),
            pltpu.VMEM((tokens // chunk, rows, chunk), F32),
            pltpu.VMEM((rows, DK), F32),
            pltpu.VMEM((heads, rows, DV), F32),
            pltpu.SemaphoreType.DMA((6,)),
        ],
        compiler_params=pltpu.CompilerParams(vmem_limit_bytes=VMEM_LIMIT),
        name="attention",
    )(q, own, other)


def output_kernel(mixed_ref, skip_ref, *rest):
    pieces, (out_ref, buf, sems) = rest[:8], rest[8:]
    copies = fill(rows_of_quarters, pieces[:4], pieces[4:], buf, sems)
    x, _ = own_place()
    tile = buf.shape[-1]
    left = mixed_ref[...]
    for i, d in enumerate((0, 3, 1, 2)):
        copies[i].wait()
        copies[4 + i].wait()
        p = lax.rem(x + d, 4)
        cols = pl.ds(pl.multiple_of(p * tile, tile), tile)
        y = jnp.dot(left, buf[p].reshape(left.shape[1], tile), preferred_element_type=F32)
        out_ref[:, cols] = (skip_ref[:, cols].astype(F32) + y).astype(BF)


def output(mixed, skip, pieces):
    rows, width = skip.shape
    return pl.pallas_call(
        output_kernel,
        out_shape=jax.ShapeDtypeStruct((rows, width), BF),
        in_specs=[IN_VMEM, IN_VMEM] + [ANYWHERE] * 8,
        scratch_shapes=[
            pltpu.VMEM((4, 8, 2, *pieces[0].shape[1:]), BF),
            pltpu.SemaphoreType.DMA((8,)),
        ],
        compiler_params=pltpu.CompilerParams(vmem_limit_bytes=VMEM_LIMIT),
        name="output",
    )(mixed, skip, *pieces)


def rotation(seq, rows):
    half = DK // 2
    freqs = jnp.power(10000.0, -jnp.arange(half, dtype=F32) / half)
    positions = seq * rows + jnp.arange(rows, dtype=jnp.int32)
    angle = positions.astype(F32)[:, None] * freqs[None, :]
    c, s = jnp.cos(angle), jnp.sin(angle)
    return jnp.concatenate([c, c], 1), jnp.concatenate([-s, s], 1)


def tied(value, *after):
    return lax.optimization_barrier((value, *after))[0]


def halos(x, seq):
    core = seq % 2
    first, last = x[:2], x[-2:]
    ends = [(l, l + 1) for l in range(128) if l % 2 and l % 16 != 15]
    outer = send(jnp.where(core == 0, first, last), ends + [(j, i) for i, j in ends])
    inner = send(jnp.where(core == 0, last, first), OTHER_CORE)
    return jnp.where(core == 0, outer, inner), jnp.where(core == 0, inner, outer)


def body(x, conv_gain, conv_weight, conv_bias, attn_gain, q_weight, kv_weight, o_weight):
    rows = x.shape[0] // 2
    seq = lax.axis_index("seq")
    qn, on = q_weight.shape[1] // 2, o_weight.shape[1] // 4
    before, after = halos(x, seq)
    block = pack(q_weight, o_weight, kv_weight)
    block, before, after = lax.optimization_barrier((block, before, after))
    block = to_same_core(block)
    skip, normed = convolve(x, before, after, conv_gain, conv_weight, conv_bias, attn_gain)
    cosine, sine = rotation(seq, rows)
    block = tied(block, normed)
    kv = key_values(
        normed, cosine, sine, block, send(block[:, :, qn + on :], OTHER_CORE)
    )
    kv_same = to_same_core(kv)
    q_own = tied(block, kv)[:, :, :qn]
    q_parts = [send(q_own[:4], along_x(1)), send(q_own[4:], along_x(-1))]
    o_own = tied(block, kv)[:, :, qn : qn + on]
    o_parts = [o_own, send(o_own, along_x(1)), send(o_own, along_x(-1))]
    o_parts.append(send(tied(o_own, *q_parts), along_x(2)))
    q = queries(normed, cosine, sine, [block, *q_parts, *swapped([q_own, *q_parts])])
    kv_same = tied(kv_same, q)
    mixed = attention(q, kv_same, send(kv_same, OTHER_CORE))
    *o_parts, mixed = lax.optimization_barrier((*o_parts, mixed))
    return skip, output(mixed, skip, o_parts + swapped(o_parts))


def solution(mesh):
    rows = P(("dp", "seq"), None)
    in_specs = (rows, P(), P(), P(), P(), P("seq", None), P("seq", None), P("seq", None))
    return jax.shard_map(
        body, mesh=mesh, in_specs=in_specs, out_specs=(rows, rows), check_vma=False
    )
```

```python
import functools
import math

import jax
import jax.numpy as jnp
from jax import lax
from jax.experimental import pallas as pl
from jax.experimental.pallas import tpu as pltpu
from jax.sharding import PartitionSpec as P

HEADS = 8
DK = 128
DV = 192
EPS = 1e-06
BF = jnp.bfloat16
F32 = jnp.float32
AXES = ("dp", "seq")
VMEM_LIMIT = 60 * 1024 * 1024
SMALL = pl.CostEstimate(flops=1000, bytes_accessed=1000, transcendentals=0)


def place(l):
    dp, s = divmod(l, 16)
    return dp // 2, dp % 2, s // 4, (s // 2) % 2, s % 2


def device(x, yl, z, yh, c):
    return ((x % 4) * 2 + yl) * 16 + (z % 4) * 4 + yh * 2 + c


def moves(f):
    return [(l, device(*f(*place(l)))) for l in range(128)]


def along_x(k):
    return moves(lambda x, yl, z, yh, c: (x + k, yl, z, yh, c))


OTHER_CORE = moves(lambda x, yl, z, yh, c: (x, yl, z, yh, 1 - c))


def send(array, pairs):
    return lax.ppermute(array, AXES, pairs)


def full(shape):
    return pl.BlockSpec(shape, lambda *_: (0,) * len(shape))


ANYWHERE = pl.BlockSpec(memory_space=pl.ANY)
IN_VMEM = pl.BlockSpec(memory_space=pltpu.VMEM)


def conv_kernel(
    x_ref, before_ref, after_ref, cg_ref, bias_ref, ag_ref, w_hbm,
    skip_ref, norm_ref, lhs, raw, wide, act_s, raw_s, w_buf, sems,
):
    n = pl.program_id(0)
    steps = pl.num_programs(0)
    rows, width = skip_ref.shape
    taps, _, tile = w_buf.shape[1:]

    def weights(i):
        cols = pl.ds(pl.multiple_of(i * tile, tile), tile)
        slot = lax.rem(i, 2)
        return pltpu.make_async_copy(w_hbm.at[:, :, cols], w_buf.at[slot], sems.at[slot])

    def activated(v):
        scale = lax.rsqrt(jnp.mean(v * v, axis=-1, keepdims=True) + EPS)
        return jax.nn.gelu(v * scale * cg_ref[...].reshape(1, width), approximate=True)

    @pl.when(n == 0)
    def _():
        weights(0).start()
        groups, some, lanes = act_s.shape

        def step(i, _):
            at = pl.multiple_of(i * some, some)
            half = pl.ds(pl.multiple_of(i * (some // 2), some // 2), some // 2)
            there = pl.ds(pl.multiple_of(i * (some // 2) + 8, 8), some // 2)
            v = x_ref[pl.ds(at, some), :].astype(F32)
            g = activated(v)
            for k in range(groups):
                cols = slice(k * lanes, (k + 1) * lanes)
                raw_s[k] = v[:, cols]
                act_s[k] = g[:, cols]
                for j in range(2):
                    a = act_s[k, pl.ds(j, some // 2, 2), :]
                    wide[j, there, cols] = a
                    lhs[2 + j, half, cols] = a.astype(BF)
                    raw[j, half, cols] = raw_s[k, pl.ds(j, some // 2, 2), :].astype(BF)
            return 0

        lax.fori_loop(0, x_ref.shape[0] // some, step, 0)
        before = activated(before_ref[...].astype(F32))
        after = activated(after_ref[...].astype(F32))
        for j in range(2):
            wide[j, 7:8, :] = before[j : j + 1]
            wide[j, rows + 8 : rows + 9, :] = after[j : j + 1]
            lhs[j] = wide[j, pl.ds(7, rows), :].astype(BF)
            lhs[4 + j] = wide[j, pl.ds(9, rows), :].astype(BF)

    @pl.when(n + 1 < steps)
    def _():
        weights(n + 1).start()

    weights(n).wait()
    slot = lax.rem(n, 2)
    acc = jnp.zeros((2 * rows, tile), F32)
    for t in range(taps):
        acc = acc + jnp.dot(
            lhs[t : t + 2].reshape(2 * rows, width), w_buf[slot, t], preferred_element_type=F32
        )
    cols = pl.ds(pl.multiple_of(n * tile, tile), tile)
    bias = bias_ref[cols].reshape(1, tile)
    even = raw[0, :, cols].astype(F32) + (acc[:rows] + bias)
    odd = raw[1, :, cols].astype(F32) + (acc[rows:] + bias)
    skip_ref[:, cols] = jnp.maximum(even, odd).astype(BF)

    @pl.when(n == steps - 1)
    def _():
        v = skip_ref[...].astype(F32)
        scale = lax.rsqrt(jnp.mean(v * v, axis=-1, keepdims=True) + EPS)
        norm_ref[...] = (v * scale * ag_ref[...].reshape(1, width)).astype(BF)


def convolve(x, before, after, conv_gain, conv_weight, conv_bias, attn_gain):
    rows, width = x.shape[0] // 2, x.shape[1]
    taps = conv_weight.shape[0]
    tile = 256
    out = jax.ShapeDtypeStruct((rows, width), BF)
    vector = full((width,))
    return pl.pallas_call(
        conv_kernel,
        out_shape=(out, out),
        grid=(width // tile,),
        in_specs=[full(x.shape), full((2, width)), full((2, width)), vector, vector, vector, ANYWHERE],
        out_specs=(full((rows, width)), full((rows, width))),
        scratch_shapes=[
            pltpu.VMEM((6, rows, width), BF),
            pltpu.VMEM((2, rows, width), BF),
            pltpu.VMEM((2, rows + 16, width), F32),
            pltpu.VMEM((width // 128, 128, 128), F32),
            pltpu.VMEM((width // 128, 128, 128), F32),
            pltpu.VMEM((2, taps, width, tile), BF),
            pltpu.SemaphoreType.DMA((2,)),
        ],
        compiler_params=pltpu.CompilerParams(vmem_limit_bytes=VMEM_LIMIT),
        cost_estimate=SMALL,
        name="conv",
    )(x, before, after, conv_gain, conv_bias, attn_gain, conv_weight)


def to_same_core(block):
    groups = [[i * 2 + c for i in range(8)] for c in range(2)]
    return lax.all_to_all(block, "seq", 0, 0, tiled=True, axis_index_groups=groups)


def swapped(pieces):
    return [send(p, OTHER_CORE) for p in pieces]


def own_place():
    return lax.axis_index("dp") // 2, lax.rem(lax.axis_index("seq"), 2)


def rows_of_quarters(buf, core):
    x, n = own_place()[0], buf.shape[-1] // 4
    return tuple(
        buf.at[:, core, :, pl.ds(pl.multiple_of(lax.rem(x + d, 4) * n, 128), n)]
        for d in (0, 3, 1, 2)
    )


def fill(rows_of, mine, theirs, buf, sems):
    c = own_place()[1]
    copies = []
    for core, pieces in ((c, mine), (1 - c, theirs)):
        for src, dst in zip(pieces, rows_of(buf, core)):
            copies.append(pltpu.make_async_copy(src, dst, sems.at[len(copies)]))
    for copy in copies:
        copy.start()
    return copies


def pack_kernel(q_hbm, o_hbm, kv_hbm, out_hbm, buf, in_sems, out_sems):
    x, _ = own_place()
    copies, at = [], 0
    for src, index, n in (
        (q_hbm, 0, q_hbm.shape[1]),
        (o_hbm, x, o_hbm.shape[1] // 4),
        (kv_hbm, 0, kv_hbm.shape[1]),
    ):
        part = src if src is not o_hbm else src.at[:, pl.ds(pl.multiple_of(index * n, 128), n)]
        copies.append(
            pltpu.make_async_copy(part, buf.at[:, pl.ds(at, n)], in_sems.at[len(copies)])
        )
        at += n
    for copy in copies:
        copy.start()
    for copy in copies:
        copy.wait()
    copies = [
        pltpu.make_async_copy(buf, out_hbm.at[i], out_sems.at[i]) for i in range(out_hbm.shape[0])
    ]
    for copy in copies:
        copy.start()
    for copy in copies:
        copy.wait()


def pack(q_weight, o_weight, kv_weight):
    rows = q_weight.shape[0]
    n = q_weight.shape[1] + o_weight.shape[1] // 4 + kv_weight.shape[1]
    return pl.pallas_call(
        pack_kernel,
        out_shape=jax.ShapeDtypeStruct((8, rows, n), BF),
        in_specs=[ANYWHERE] * 3,
        out_specs=ANYWHERE,
        scratch_shapes=[
            pltpu.VMEM((rows, n), BF),
            pltpu.SemaphoreType.DMA((3,)),
            pltpu.SemaphoreType.DMA((8,)),
        ],
        compiler_params=pltpu.CompilerParams(vmem_limit_bytes=VMEM_LIMIT),
        cost_estimate=SMALL,
        name="pack",
    )(q_weight, o_weight, kv_weight)


def rotated(v, c, s):
    return v * c + pltpu.roll(v, DK // 2, 1) * s


def kv_kernel(norm_ref, cos_ref, sin_ref, own, other, kv_ref, q_ref, o_ref, buf, sems):
    _, c = own_place()
    qn, on, n = q_ref.shape[2], o_ref.shape[2], other.shape[2]
    copies = [
        pltpu.make_async_copy(own.at[:, :, pl.ds(qn + on, n)], buf.at[:, c], sems.at[0]),
        pltpu.make_async_copy(other, buf.at[:, 1 - c], sems.at[1]),
        pltpu.make_async_copy(own.at[:, :, pl.ds(0, qn)], q_ref, sems.at[2]),
        pltpu.make_async_copy(own.at[:, :, pl.ds(qn, on)], o_ref, sems.at[3]),
    ]
    for copy in copies:
        copy.start()
    for copy in copies[:2]:
        copy.wait()
    x = norm_ref[...]
    rows, width = x.shape
    kv = jnp.dot(x, buf[...].reshape(width, buf.shape[-1]), preferred_element_type=F32)
    tail = kv[:, 2 * DK :]
    packed = jnp.concatenate(
        [
            rotated(kv[:, :DK], cos_ref[...], sin_ref[...]),
            kv[:, DK : 2 * DK],
            jnp.concatenate([tail[: rows // 2], tail[rows // 2 :]], axis=1),
        ],
        axis=0,
    ).astype(BF)
    for i in range(kv_ref.shape[0]):
        kv_ref[i] = packed
    for copy in copies[2:]:
        copy.wait()


def key_values(normed, cosine, sine, own, other, qn, on):
    rows = normed.shape[0]
    return pl.pallas_call(
        kv_kernel,
        out_shape=(
            jax.ShapeDtypeStruct((8, rows * 5 // 2, DK), BF),
            jax.ShapeDtypeStruct((*own.shape[:2], qn), BF),
            jax.ShapeDtypeStruct((*own.shape[:2], on), BF),
        ),
        in_specs=[IN_VMEM, IN_VMEM, IN_VMEM, ANYWHERE, ANYWHERE],
        out_specs=(IN_VMEM, IN_VMEM, IN_VMEM),
        scratch_shapes=[
            pltpu.VMEM((8, 2, *other.shape[1:]), BF),
            pltpu.SemaphoreType.DMA((4,)),
        ],
        compiler_params=pltpu.CompilerParams(vmem_limit_bytes=VMEM_LIMIT),
        cost_estimate=SMALL,
        name="key_values",
    )(normed, cosine, sine, own, other)


def query_kernel(norm_ref, cos_ref, sin_ref, own, other, q_ref, buf, sems):
    _, core = own_place()
    copies = [
        pltpu.make_async_copy(own, buf.at[:, core], sems.at[0]),
        pltpu.make_async_copy(other, buf.at[:, 1 - core], sems.at[1]),
    ]
    for copy in copies:
        copy.start()
    for copy in copies:
        copy.wait()
    x = norm_ref[...]
    c, s = cos_ref[...], sin_ref[...]
    y = jnp.dot(x, buf[...].reshape(x.shape[1], buf.shape[-1]), preferred_element_type=F32)
    for h in range(HEADS):
        q_ref[h] = rotated(y[:, h * DK : (h + 1) * DK], c, s).astype(BF)


def queries(normed, cosine, sine, own, other):
    rows, _ = normed.shape
    return pl.pallas_call(
        query_kernel,
        out_shape=jax.ShapeDtypeStruct((HEADS, rows, DK), BF),
        in_specs=[IN_VMEM, IN_VMEM, IN_VMEM, ANYWHERE, ANYWHERE],
        scratch_shapes=[
            pltpu.VMEM((8, 2, *other.shape[1:]), BF),
            pltpu.SemaphoreType.DMA((2,)),
        ],
        compiler_params=pltpu.CompilerParams(vmem_limit_bytes=VMEM_LIMIT),
        cost_estimate=SMALL,
        name="queries",
    )(normed, cosine, sine, own, other)


def attention_kernel(
    q_ref, own, other, out_ref, kbuf, vbuf, tails, even_s, odd_s, peak, heads_s, sems
):
    heads, rows, _ = q_ref.shape
    slabs = kbuf.shape[0]
    half = rows // 2
    copies = []
    for i, part in enumerate((own, other)):
        to = pl.ds(i * (slabs // 2), slabs // 2)
        for lo, size, dst in (
            (0, rows, kbuf.at[to]),
            (rows, rows, vbuf.at[to, :, pl.ds(0, DK)]),
            (2 * rows, half, tails.at[to]),
        ):
            copies.append(
                pltpu.make_async_copy(part.at[:, pl.ds(lo, size), :], dst, sems.at[len(copies)])
            )
    for i in (0, 3, 1, 2, 4, 5):
        copies[i].start()
    copies[0].wait()
    copies[3].wait()
    chunks, _, chunk = even_s.shape
    n = chunk // rows
    scale = DK ** (-0.5) * math.log2(math.e)
    lowest = jnp.full((rows, DK), -jnp.inf, F32)

    def make_scores(head, to):
        top = lowest
        for kc in range(chunks):
            k = kbuf[kc * n : (kc + 1) * n].reshape(chunk, DK)
            s = lax.dot_general(
                q_ref[head], k, (((1,), (1,)), ((), ())), preferred_element_type=F32
            )
            to[kc] = s
            for j in range(chunk // DK):
                top = jnp.maximum(top, s[:, j * DK : (j + 1) * DK])
        return jnp.broadcast_to(jnp.max(top, axis=-1, keepdims=True), (rows, DK))

    def use_scores(head, scores, m):
        total = jnp.zeros((rows, 2 * DK), F32)
        for kc in range(chunks):
            s = scores[kc]
            w = jnp.concatenate(
                [jnp.exp2((s[:, j * DK : (j + 1) * DK] - m) * scale) for j in range(chunk // DK)],
                axis=1,
            ).astype(BF)
            v = vbuf[kc * n : (kc + 1) * n].reshape(chunk, 2 * DK)
            total = total + jnp.dot(w, v, preferred_element_type=F32)
        heads_s[head] = total[:, :DV] / total[:, DV : DV + 1]

    peak[...] = make_scores(0, even_s)
    for i in (1, 2, 4, 5):
        copies[i].wait()
    lane = lax.broadcasted_iota(jnp.int32, (half, DK), 1)
    ones = jnp.where(lane == DK // 2, 1.0, 0.0)
    for i in range(slabs):
        t = tails[i].astype(F32)
        vbuf[i, :half, DK:] = jnp.where(lane < DK // 2, t, ones).astype(BF)
        vbuf[i, half:, DK:] = jnp.where(
            lane < DK // 2, pltpu.roll(t, DK // 2, 1), ones
        ).astype(BF)

    def step(i, _):
        head = 2 * i
        m = peak[...]
        above = make_scores(head + 1, odd_s)
        use_scores(head, even_s, m)
        peak[...] = make_scores(head + 2, even_s)
        use_scores(head + 1, odd_s, above)
        return 0

    lax.fori_loop(0, heads // 2 - 1, step, 0)
    m = peak[...]
    above = make_scores(heads - 1, odd_s)
    use_scores(heads - 2, even_s, m)
    use_scores(heads - 1, odd_s, above)
    for h in range(0, heads, 2):
        out_ref[:, h * DV : (h + 2) * DV] = jnp.concatenate(
            [heads_s[h], heads_s[h + 1]], axis=1
        ).astype(BF)


def attention(q, own, other):
    heads, rows, _ = q.shape
    slabs = 2 * own.shape[0]
    tokens = slabs * rows
    chunk = 2048
    return pl.pallas_call(
        attention_kernel,
        out_shape=jax.ShapeDtypeStruct((rows, heads * DV), BF),
        in_specs=[IN_VMEM, ANYWHERE, ANYWHERE],
        scratch_shapes=[
            pltpu.VMEM((slabs, rows, DK), BF),
            pltpu.VMEM((slabs, rows, 2 * DK), BF),
            pltpu.VMEM((slabs, rows // 2, DK), BF),
            pltpu.VMEM((tokens // chunk, rows, chunk), F32),
            pltpu.VMEM((tokens // chunk, rows, chunk), F32),
            pltpu.VMEM((rows, DK), F32),
            pltpu.VMEM((heads, rows, DV), F32),
            pltpu.SemaphoreType.DMA((6,)),
        ],
        compiler_params=pltpu.CompilerParams(vmem_limit_bytes=VMEM_LIMIT),
        cost_estimate=SMALL,
        name="attention",
    )(q, own, other)


def output_kernel(mixed_ref, skip_ref, *rest):
    pieces, (out_ref, buf, sems) = rest[:8], rest[8:]
    for copy in fill(rows_of_quarters, pieces[:4], pieces[4:], buf, sems):
        copy.wait()
    left = mixed_ref[...]
    y = jnp.dot(left, buf[...].reshape(left.shape[1], buf.shape[-1]), preferred_element_type=F32)
    out_ref[...] = (skip_ref[...].astype(F32) + y).astype(BF)


def output(mixed, skip, pieces):
    rows, width = skip.shape
    return pl.pallas_call(
        output_kernel,
        out_shape=jax.ShapeDtypeStruct((rows, width), BF),
        in_specs=[IN_VMEM, IN_VMEM] + [ANYWHERE] * 8,
        scratch_shapes=[
            pltpu.VMEM((8, 2, pieces[0].shape[1], width), BF),
            pltpu.SemaphoreType.DMA((8,)),
        ],
        compiler_params=pltpu.CompilerParams(vmem_limit_bytes=VMEM_LIMIT),
        cost_estimate=SMALL,
        name="output",
    )(mixed, skip, *pieces)


def rotation(seq, rows):
    half = DK // 2
    freqs = jnp.power(10000.0, -jnp.arange(half, dtype=F32) / half)
    positions = seq * rows + jnp.arange(rows, dtype=jnp.int32)
    angle = positions.astype(F32)[:, None] * freqs[None, :]
    c, s = jnp.cos(angle), jnp.sin(angle)
    return jnp.concatenate([c, c], 1), jnp.concatenate([-s, s], 1)


def tied(value, *after):
    return lax.optimization_barrier((value, *after))[0]


def halos(x, seq):
    core = seq % 2
    first, last = x[:2], x[-2:]
    ends = [(l, l + 1) for l in range(128) if l % 2 and l % 16 != 15]
    outer = send(jnp.where(core == 0, first, last), ends + [(j, i) for i, j in ends])
    inner = send(jnp.where(core == 0, last, first), OTHER_CORE)
    return jnp.where(core == 0, outer, inner), jnp.where(core == 0, inner, outer)


def body(x, conv_gain, conv_weight, conv_bias, attn_gain, q_weight, kv_weight, o_weight):
    rows = x.shape[0] // 2
    seq = lax.axis_index("seq")
    qn, on = q_weight.shape[1], o_weight.shape[1] // 4
    before, after = halos(x, seq)
    block = pack(q_weight, o_weight, kv_weight)
    block, before, after = lax.optimization_barrier((block, before, after))
    block = to_same_core(block)
    skip, normed = convolve(x, before, after, conv_gain, conv_weight, conv_bias, attn_gain)
    cosine, sine = rotation(seq, rows)
    block = tied(block, normed)
    kv, q_own, o_own = key_values(
        normed, cosine, sine, block, send(block[:, :, qn + on :], OTHER_CORE), qn, on
    )
    kv_same = to_same_core(kv)
    o_parts = [o_own, *(send(o_own, along_x(k)) for k in (1, -1, 2))]
    q = queries(normed, cosine, sine, q_own, send(q_own, OTHER_CORE))
    kv_same = tied(kv_same, q, *o_parts[1:3])
    mixed = attention(q, kv_same, send(kv_same, OTHER_CORE))
    o_other = swapped(o_parts[:3]) + swapped([tied(o_parts[3], mixed)])
    return skip, output(mixed, skip, o_parts + o_other)


def solution(mesh):
    rows = P(("dp", "seq"), None)
    in_specs = (rows, P(), P(), P(), P(), P("seq", None), P("seq", None), P("seq", None))
    return jax.shard_map(
        body, mesh=mesh, in_specs=in_specs, out_specs=(rows, rows), check_vma=False
    )
```

```python
import functools
import math

import jax
import jax.numpy as jnp
from jax import lax
from jax.experimental import pallas as pl
from jax.experimental.pallas import tpu as pltpu
from jax.sharding import PartitionSpec as P

HEADS = 8
DK = 128
DV = 192
EPS = 1e-06
BF = jnp.bfloat16
F32 = jnp.float32
AXES = ("dp", "seq")
MIB = 1024 * 1024
VMEM_LIMIT = 60 * MIB
SMALL = pl.CostEstimate(flops=1000, bytes_accessed=1000, transcendentals=0)


def place(l):
    dp, s = divmod(l, 16)
    return dp // 2, dp % 2, s // 4, (s // 2) % 2, s % 2


def device(x, yl, z, yh, c):
    return ((x % 4) * 2 + yl) * 16 + (z % 4) * 4 + yh * 2 + c


def moves(f):
    return [(l, device(*f(*place(l)))) for l in range(128)]


def along_x(k):
    return moves(lambda x, yl, z, yh, c: (x + k, yl, z, yh, c))


OTHER_CORE = moves(lambda x, yl, z, yh, c: (x, yl, z, yh, 1 - c))


def send(array, pairs):
    return lax.ppermute(array, AXES, pairs)


def full(shape):
    return pl.BlockSpec(shape, lambda *_: (0,) * len(shape))


ANYWHERE = pl.BlockSpec(memory_space=pl.ANY)
IN_VMEM = pl.BlockSpec(memory_space=pltpu.VMEM)


def conv_kernel(
    x_ref, before_ref, after_ref, cg_ref, bias_ref, ag_ref, w_hbm,
    skip_ref, norm_ref, lhs, raw, wide, act_s, raw_s, w_buf, sems,
):
    n = pl.program_id(0)
    steps = pl.num_programs(0)
    rows, width = skip_ref.shape
    taps, _, tile = w_buf.shape[1:]

    def weights(i):
        cols = pl.ds(pl.multiple_of(i * tile, tile), tile)
        slot = lax.rem(i, 2)
        return pltpu.make_async_copy(w_hbm.at[:, :, cols], w_buf.at[slot], sems.at[slot])

    def activated(v):
        scale = lax.rsqrt(jnp.mean(v * v, axis=-1, keepdims=True) + EPS)
        return jax.nn.gelu(v * scale * cg_ref[...].reshape(1, width), approximate=True)

    @pl.when(n == 0)
    def _():
        weights(0).start()
        groups, some, lanes = act_s.shape

        def step(i, _):
            at = pl.multiple_of(i * some, some)
            half = pl.ds(pl.multiple_of(i * (some // 2), some // 2), some // 2)
            there = pl.ds(pl.multiple_of(i * (some // 2) + 8, 8), some // 2)
            v = x_ref[pl.ds(at, some), :].astype(F32)
            g = activated(v)
            for k in range(groups):
                cols = slice(k * lanes, (k + 1) * lanes)
                raw_s[k] = v[:, cols]
                act_s[k] = g[:, cols]
                for j in range(2):
                    a = act_s[k, pl.ds(j, some // 2, 2), :]
                    wide[j, there, cols] = a
                    lhs[2 + j, half, cols] = a.astype(BF)
                    raw[j, half, cols] = raw_s[k, pl.ds(j, some // 2, 2), :].astype(BF)
            return 0

        lax.fori_loop(0, x_ref.shape[0] // some, step, 0)
        before = activated(before_ref[...].astype(F32))
        after = activated(after_ref[...].astype(F32))
        for j in range(2):
            wide[j, 7:8, :] = before[j : j + 1]
            wide[j, rows + 8 : rows + 9, :] = after[j : j + 1]
            lhs[j] = wide[j, pl.ds(7, rows), :].astype(BF)
            lhs[4 + j] = wide[j, pl.ds(9, rows), :].astype(BF)

    @pl.when(n + 1 < steps)
    def _():
        weights(n + 1).start()

    weights(n).wait()
    slot = lax.rem(n, 2)
    acc = jnp.zeros((2 * rows, tile), F32)
    for t in range(taps):
        acc = acc + jnp.dot(
            lhs[t : t + 2].reshape(2 * rows, width), w_buf[slot, t], preferred_element_type=F32
        )
    cols = pl.ds(pl.multiple_of(n * tile, tile), tile)
    bias = bias_ref[cols].reshape(1, tile)
    even = raw[0, :, cols].astype(F32) + (acc[:rows] + bias)
    odd = raw[1, :, cols].astype(F32) + (acc[rows:] + bias)
    skip_ref[:, cols] = jnp.maximum(even, odd).astype(BF)

    @pl.when(n == steps - 1)
    def _():
        v = skip_ref[...].astype(F32)
        scale = lax.rsqrt(jnp.mean(v * v, axis=-1, keepdims=True) + EPS)
        norm_ref[...] = (v * scale * ag_ref[...].reshape(1, width)).astype(BF)


def convolve(x, before, after, conv_gain, conv_weight, conv_bias, attn_gain):
    rows, width = x.shape[0] // 2, x.shape[1]
    taps = conv_weight.shape[0]
    tile = 256
    out = jax.ShapeDtypeStruct((rows, width), BF)
    vector = full((width,))
    return pl.pallas_call(
        conv_kernel,
        out_shape=(out, out),
        grid=(width // tile,),
        in_specs=[full(x.shape), full((2, width)), full((2, width)), vector, vector, vector, ANYWHERE],
        out_specs=(full((rows, width)), full((rows, width))),
        scratch_shapes=[
            pltpu.VMEM((6, rows, width), BF),
            pltpu.VMEM((2, rows, width), BF),
            pltpu.VMEM((2, rows + 16, width), F32),
            pltpu.VMEM((width // 128, 128, 128), F32),
            pltpu.VMEM((width // 128, 128, 128), F32),
            pltpu.VMEM((2, taps, width, tile), BF),
            pltpu.SemaphoreType.DMA((2,)),
        ],
        compiler_params=pltpu.CompilerParams(vmem_limit_bytes=36 * MIB),
        cost_estimate=SMALL,
        name="conv",
    )(x, before, after, conv_gain, conv_bias, attn_gain, conv_weight)


def to_same_core(block):
    groups = [[i * 2 + c for i in range(8)] for c in range(2)]
    return lax.all_to_all(block, "seq", 0, 0, tiled=True, axis_index_groups=groups)


def swapped(pieces):
    return [send(p, OTHER_CORE) for p in pieces]


def own_place():
    return lax.axis_index("dp") // 2, lax.rem(lax.axis_index("seq"), 2)


def rows_of_quarters(buf, core):
    x, n = own_place()[0], buf.shape[-1] // 4
    return tuple(
        buf.at[:, core, :, pl.ds(pl.multiple_of(lax.rem(x + d, 4) * n, 128), n)]
        for d in (0, 3, 1, 2)
    )


def fill(rows_of, mine, theirs, buf, sems):
    c = own_place()[1]
    copies = []
    for core, pieces in ((c, mine), (1 - c, theirs)):
        for src, dst in zip(pieces, rows_of(buf, core)):
            copies.append(pltpu.make_async_copy(src, dst, sems.at[len(copies)]))
    for copy in copies:
        copy.start()
    return copies


def pack_kernel(q_hbm, o_hbm, kv_hbm, out_hbm, buf, in_sems, out_sems):
    x, _ = own_place()
    copies, at = [], 0
    for src, index, n in (
        (q_hbm, 0, q_hbm.shape[1]),
        (o_hbm, x, o_hbm.shape[1] // 4),
        (kv_hbm, 0, kv_hbm.shape[1]),
    ):
        part = src if src is not o_hbm else src.at[:, pl.ds(pl.multiple_of(index * n, 128), n)]
        copies.append(
            pltpu.make_async_copy(part, buf.at[:, pl.ds(at, n)], in_sems.at[len(copies)])
        )
        at += n
    for copy in copies:
        copy.start()
    for copy in copies:
        copy.wait()
    copies = [
        pltpu.make_async_copy(buf, out_hbm.at[i], out_sems.at[i]) for i in range(out_hbm.shape[0])
    ]
    for copy in copies:
        copy.start()
    for copy in copies:
        copy.wait()


def pack(q_weight, o_weight, kv_weight):
    rows = q_weight.shape[0]
    n = q_weight.shape[1] + o_weight.shape[1] // 4 + kv_weight.shape[1]
    return pl.pallas_call(
        pack_kernel,
        out_shape=jax.ShapeDtypeStruct((8, rows, n), BF),
        in_specs=[ANYWHERE] * 3,
        out_specs=ANYWHERE,
        scratch_shapes=[
            pltpu.VMEM((rows, n), BF),
            pltpu.SemaphoreType.DMA((3,)),
            pltpu.SemaphoreType.DMA((8,)),
        ],
        compiler_params=pltpu.CompilerParams(vmem_limit_bytes=VMEM_LIMIT),
        cost_estimate=SMALL,
        name="pack",
    )(q_weight, o_weight, kv_weight)


def rotated(v, c, s):
    return v * c + pltpu.roll(v, DK // 2, 1) * s


def kv_kernel(norm_ref, cos_ref, sin_ref, own, other, kv_ref, q_ref, o_ref, buf, sems):
    _, c = own_place()
    qn, on, n = q_ref.shape[2], o_ref.shape[2], other.shape[2]
    copies = [
        pltpu.make_async_copy(own.at[:, :, pl.ds(qn + on, n)], buf.at[:, c], sems.at[0]),
        pltpu.make_async_copy(other, buf.at[:, 1 - c], sems.at[1]),
        pltpu.make_async_copy(own.at[:, :, pl.ds(0, qn)], q_ref, sems.at[2]),
        pltpu.make_async_copy(own.at[:, :, pl.ds(qn, on)], o_ref, sems.at[3]),
    ]
    for copy in copies:
        copy.start()
    for copy in copies[:2]:
        copy.wait()
    x = norm_ref[...]
    rows, width = x.shape
    kv = jnp.dot(x, buf[...].reshape(width, buf.shape[-1]), preferred_element_type=F32)
    tail = kv[:, 2 * DK :]
    packed = jnp.concatenate(
        [
            rotated(kv[:, :DK], cos_ref[...], sin_ref[...]),
            kv[:, DK : 2 * DK],
            jnp.concatenate([tail[: rows // 2], tail[rows // 2 :]], axis=1),
        ],
        axis=0,
    ).astype(BF)
    for i in range(kv_ref.shape[0]):
        kv_ref[i] = packed
    for copy in copies[2:]:
        copy.wait()


def key_values(normed, cosine, sine, own, other, qn, on):
    rows = normed.shape[0]
    return pl.pallas_call(
        kv_kernel,
        out_shape=(
            jax.ShapeDtypeStruct((8, rows * 5 // 2, DK), BF),
            jax.ShapeDtypeStruct((*own.shape[:2], qn), BF),
            jax.ShapeDtypeStruct((*own.shape[:2], on), BF),
        ),
        in_specs=[IN_VMEM, IN_VMEM, IN_VMEM, ANYWHERE, ANYWHERE],
        out_specs=(IN_VMEM, IN_VMEM, IN_VMEM),
        scratch_shapes=[
            pltpu.VMEM((8, 2, *other.shape[1:]), BF),
            pltpu.SemaphoreType.DMA((4,)),
        ],
        compiler_params=pltpu.CompilerParams(vmem_limit_bytes=16 * MIB),
        cost_estimate=SMALL,
        name="key_values",
    )(normed, cosine, sine, own, other)


def query_kernel(norm_ref, cos_ref, sin_ref, own, other, q_ref, buf, sems):
    _, core = own_place()
    copies = [
        pltpu.make_async_copy(own, buf.at[:, core], sems.at[0]),
        pltpu.make_async_copy(other, buf.at[:, 1 - core], sems.at[1]),
    ]
    for copy in copies:
        copy.start()
    for copy in copies:
        copy.wait()
    x = norm_ref[...]
    c, s = cos_ref[...], sin_ref[...]
    y = jnp.dot(x, buf[...].reshape(x.shape[1], buf.shape[-1]), preferred_element_type=F32)
    for h in range(HEADS):
        q_ref[h] = rotated(y[:, h * DK : (h + 1) * DK], c, s).astype(BF)


def queries(normed, cosine, sine, own, other):
    rows, _ = normed.shape
    return pl.pallas_call(
        query_kernel,
        out_shape=jax.ShapeDtypeStruct((HEADS, rows, DK), BF),
        in_specs=[IN_VMEM, IN_VMEM, IN_VMEM, ANYWHERE, ANYWHERE],
        scratch_shapes=[
            pltpu.VMEM((8, 2, *other.shape[1:]), BF),
            pltpu.SemaphoreType.DMA((2,)),
        ],
        compiler_params=pltpu.CompilerParams(vmem_limit_bytes=16 * MIB),
        cost_estimate=SMALL,
        name="queries",
    )(normed, cosine, sine, own, other)


def attention_kernel(
    q_ref, own, other, out_ref, kbuf, vbuf, tails, even_s, odd_s, peak, heads_s, sems
):
    heads, rows, _ = q_ref.shape
    slabs = kbuf.shape[0]
    half = rows // 2
    copies = []
    for i, part in enumerate((own, other)):
        to = pl.ds(i * (slabs // 2), slabs // 2)
        for lo, size, dst in (
            (0, rows, kbuf.at[to]),
            (rows, rows, vbuf.at[to, :, pl.ds(0, DK)]),
            (2 * rows, half, tails.at[to]),
        ):
            copies.append(
                pltpu.make_async_copy(part.at[:, pl.ds(lo, size), :], dst, sems.at[len(copies)])
            )
    for i in (0, 3, 1, 2, 4, 5):
        copies[i].start()
    copies[0].wait()
    copies[3].wait()
    chunks, _, chunk = even_s.shape
    n = chunk // rows
    scale = DK ** (-0.5) * math.log2(math.e)
    lowest = jnp.full((rows, DK), -jnp.inf, F32)

    def make_scores(head, to):
        top = lowest
        for kc in range(chunks):
            k = kbuf[kc * n : (kc + 1) * n].reshape(chunk, DK)
            s = lax.dot_general(
                q_ref[head], k, (((1,), (1,)), ((), ())), preferred_element_type=F32
            )
            to[kc] = s
            for j in range(chunk // DK):
                top = jnp.maximum(top, s[:, j * DK : (j + 1) * DK])
        return jnp.broadcast_to(jnp.max(top, axis=-1, keepdims=True), (rows, DK))

    def use_scores(head, scores, m):
        total = jnp.zeros((rows, 2 * DK), F32)
        for kc in range(chunks):
            s = scores[kc]
            w = jnp.concatenate(
                [jnp.exp2((s[:, j * DK : (j + 1) * DK] - m) * scale) for j in range(chunk // DK)],
                axis=1,
            ).astype(BF)
            v = vbuf[kc * n : (kc + 1) * n].reshape(chunk, 2 * DK)
            total = total + jnp.dot(w, v, preferred_element_type=F32)
        heads_s[head] = total[:, :DV] / total[:, DV : DV + 1]

    peak[...] = make_scores(0, even_s)
    for i in (1, 2, 4, 5):
        copies[i].wait()
    lane = lax.broadcasted_iota(jnp.int32, (half, DK), 1)
    ones = jnp.where(lane == DK // 2, 1.0, 0.0)
    for i in range(slabs):
        t = tails[i].astype(F32)
        vbuf[i, :half, DK:] = jnp.where(lane < DK // 2, t, ones).astype(BF)
        vbuf[i, half:, DK:] = jnp.where(
            lane < DK // 2, pltpu.roll(t, DK // 2, 1), ones
        ).astype(BF)

    def step(i, _):
        head = 2 * i
        m = peak[...]
        above = make_scores(head + 1, odd_s)
        use_scores(head, even_s, m)
        peak[...] = make_scores(head + 2, even_s)
        use_scores(head + 1, odd_s, above)
        return 0

    lax.fori_loop(0, heads // 2 - 1, step, 0)
    m = peak[...]
    above = make_scores(heads - 1, odd_s)
    use_scores(heads - 2, even_s, m)
    use_scores(heads - 1, odd_s, above)
    for h in range(0, heads, 2):
        out_ref[:, h * DV : (h + 2) * DV] = jnp.concatenate(
            [heads_s[h], heads_s[h + 1]], axis=1
        ).astype(BF)


def attention(q, own, other):
    heads, rows, _ = q.shape
    slabs = 2 * own.shape[0]
    tokens = slabs * rows
    chunk = 2048
    return pl.pallas_call(
        attention_kernel,
        out_shape=jax.ShapeDtypeStruct((rows, heads * DV), BF),
        in_specs=[IN_VMEM, ANYWHERE, ANYWHERE],
        scratch_shapes=[
            pltpu.VMEM((slabs, rows, DK), BF),
            pltpu.VMEM((slabs, rows, 2 * DK), BF),
            pltpu.VMEM((slabs, rows // 2, DK), BF),
            pltpu.VMEM((tokens // chunk, rows, chunk), F32),
            pltpu.VMEM((tokens // chunk, rows, chunk), F32),
            pltpu.VMEM((rows, DK), F32),
            pltpu.VMEM((heads, rows, DV), F32),
            pltpu.SemaphoreType.DMA((6,)),
        ],
        compiler_params=pltpu.CompilerParams(vmem_limit_bytes=32 * MIB),
        cost_estimate=SMALL,
        name="attention",
    )(q, own, other)


def output_kernel(mixed_ref, skip_ref, *rest):
    pieces, (out_ref, buf, sems) = rest[:8], rest[8:]
    for copy in fill(rows_of_quarters, pieces[:4], pieces[4:], buf, sems):
        copy.wait()
    left = mixed_ref[...]
    y = jnp.dot(left, buf[...].reshape(left.shape[1], buf.shape[-1]), preferred_element_type=F32)
    out_ref[...] = (skip_ref[...].astype(F32) + y).astype(BF)


def output(mixed, skip, pieces):
    rows, width = skip.shape
    return pl.pallas_call(
        output_kernel,
        out_shape=jax.ShapeDtypeStruct((rows, width), BF),
        in_specs=[IN_VMEM, IN_VMEM] + [ANYWHERE] * 8,
        scratch_shapes=[
            pltpu.VMEM((8, 2, pieces[0].shape[1], width), BF),
            pltpu.SemaphoreType.DMA((8,)),
        ],
        compiler_params=pltpu.CompilerParams(vmem_limit_bytes=16 * MIB),
        cost_estimate=SMALL,
        name="output",
    )(mixed, skip, *pieces)


def rotation(seq, rows):
    half = DK // 2
    freqs = jnp.power(10000.0, -jnp.arange(half, dtype=F32) / half)
    positions = seq * rows + jnp.arange(rows, dtype=jnp.int32)
    angle = positions.astype(F32)[:, None] * freqs[None, :]
    c, s = jnp.cos(angle), jnp.sin(angle)
    return jnp.concatenate([c, c], 1), jnp.concatenate([-s, s], 1)


def tied(value, *after):
    return lax.optimization_barrier((value, *after))[0]


def halos(x, seq):
    core = seq % 2
    first, last = x[:2], x[-2:]
    ends = [(l, l + 1) for l in range(128) if l % 2 and l % 16 != 15]
    outer = send(jnp.where(core == 0, first, last), ends + [(j, i) for i, j in ends])
    inner = send(jnp.where(core == 0, last, first), OTHER_CORE)
    return jnp.where(core == 0, outer, inner), jnp.where(core == 0, inner, outer)


def body(x, conv_gain, conv_weight, conv_bias, attn_gain, q_weight, kv_weight, o_weight):
    rows = x.shape[0] // 2
    seq = lax.axis_index("seq")
    qn, on = q_weight.shape[1], o_weight.shape[1] // 4
    before, after = halos(x, seq)
    block = pack(q_weight, o_weight, kv_weight)
    block, before, after = lax.optimization_barrier((block, before, after))
    block = to_same_core(block)
    skip, normed = convolve(x, before, after, conv_gain, conv_weight, conv_bias, attn_gain)
    cosine, sine = rotation(seq, rows)
    block = tied(block, normed)
    kv, q_own, o_own = key_values(
        normed, cosine, sine, block, send(block[:, :, qn + on :], OTHER_CORE), qn, on
    )
    kv_same = to_same_core(kv)
    o_parts = [o_own, *(send(o_own, along_x(k)) for k in (1, -1, 2))]
    q = queries(normed, cosine, sine, q_own, send(q_own, OTHER_CORE))
    kv_same = tied(kv_same, q, *o_parts[1:3])
    mixed = attention(q, kv_same, send(kv_same, OTHER_CORE))
    o_other = swapped(o_parts[:3]) + swapped([tied(o_parts[3], mixed)])
    return skip, output(mixed, skip, o_parts + o_other)


def solution(mesh):
    rows = P(("dp", "seq"), None)
    in_specs = (rows, P(), P(), P(), P(), P("seq", None), P("seq", None), P("seq", None))
    return jax.shard_map(
        body, mesh=mesh, in_specs=in_specs, out_specs=(rows, rows), check_vma=False
    )
```

```python
import functools
import math

import jax
import jax.numpy as jnp
from jax import lax
from jax.experimental import pallas as pl
from jax.experimental.pallas import tpu as pltpu
from jax.sharding import PartitionSpec as P

HEADS = 8
DK = 128
DV = 192
EPS = 1e-06
BF = jnp.bfloat16
F32 = jnp.float32
AXES = ("dp", "seq")
MIB = 1024 * 1024
VMEM_LIMIT = 60 * MIB
SMALL = pl.CostEstimate(flops=1000, bytes_accessed=1000, transcendentals=0)


def place(l):
    dp, s = divmod(l, 16)
    return dp // 2, dp % 2, s // 4, (s // 2) % 2, s % 2


def device(x, yl, z, yh, c):
    return ((x % 4) * 2 + yl) * 16 + (z % 4) * 4 + yh * 2 + c


def moves(f):
    return [(l, device(*f(*place(l)))) for l in range(128)]


def along_x(k):
    return moves(lambda x, yl, z, yh, c: (x + k, yl, z, yh, c))


OTHER_CORE = moves(lambda x, yl, z, yh, c: (x, yl, z, yh, 1 - c))


def send(array, pairs):
    return lax.ppermute(array, AXES, pairs)


def full(shape):
    return pl.BlockSpec(shape, lambda *_: (0,) * len(shape))


ANYWHERE = pl.BlockSpec(memory_space=pl.ANY)
IN_VMEM = pl.BlockSpec(memory_space=pltpu.VMEM)


def conv_kernel(
    x_ref, before_ref, after_ref, cg_ref, bias_ref, ag_ref, w_hbm,
    skip_ref, norm_ref, lhs, raw, wide, act_s, raw_s, w_buf, sems,
):
    n = pl.program_id(0)
    steps = pl.num_programs(0)
    rows, width = skip_ref.shape
    taps, _, tile = w_buf.shape[1:]

    def weights(i):
        cols = pl.ds(pl.multiple_of(i * tile, tile), tile)
        slot = lax.rem(i, 2)
        return pltpu.make_async_copy(w_hbm.at[:, :, cols], w_buf.at[slot], sems.at[slot])

    def activated(v):
        scale = lax.rsqrt(jnp.mean(v * v, axis=-1, keepdims=True) + EPS)
        return jax.nn.gelu(v * scale * cg_ref[...].reshape(1, width), approximate=True)

    @pl.when(n == 0)
    def _():
        weights(0).start()
        groups, some, lanes = act_s.shape

        def step(i, _):
            at = pl.multiple_of(i * some, some)
            half = pl.ds(pl.multiple_of(i * (some // 2), some // 2), some // 2)
            there = pl.ds(pl.multiple_of(i * (some // 2) + 8, 8), some // 2)
            v = x_ref[pl.ds(at, some), :].astype(F32)
            g = activated(v)
            for k in range(groups):
                cols = slice(k * lanes, (k + 1) * lanes)
                raw_s[k] = v[:, cols]
                act_s[k] = g[:, cols]
                for j in range(2):
                    a = act_s[k, pl.ds(j, some // 2, 2), :]
                    wide[j, there, cols] = a
                    lhs[2 + j, half, cols] = a.astype(BF)
                    raw[j, half, cols] = raw_s[k, pl.ds(j, some // 2, 2), :].astype(BF)
            return 0

        lax.fori_loop(0, x_ref.shape[0] // some, step, 0)
        before = activated(before_ref[...].astype(F32))
        after = activated(after_ref[...].astype(F32))
        for j in range(2):
            wide[j, 7:8, :] = before[j : j + 1]
            wide[j, rows + 8 : rows + 9, :] = after[j : j + 1]
            lhs[j] = wide[j, pl.ds(7, rows), :].astype(BF)
            lhs[4 + j] = wide[j, pl.ds(9, rows), :].astype(BF)

    @pl.when(n + 1 < steps)
    def _():
        weights(n + 1).start()

    weights(n).wait()
    slot = lax.rem(n, 2)
    acc = jnp.zeros((2 * rows, tile), F32)
    for t in range(taps):
        acc = acc + jnp.dot(
            lhs[t : t + 2].reshape(2 * rows, width), w_buf[slot, t], preferred_element_type=F32
        )
    cols = pl.ds(pl.multiple_of(n * tile, tile), tile)
    bias = bias_ref[cols].reshape(1, tile)
    even = raw[0, :, cols].astype(F32) + (acc[:rows] + bias)
    odd = raw[1, :, cols].astype(F32) + (acc[rows:] + bias)
    skip_ref[:, cols] = jnp.maximum(even, odd).astype(BF)

    @pl.when(n == steps - 1)
    def _():
        v = skip_ref[...].astype(F32)
        scale = lax.rsqrt(jnp.mean(v * v, axis=-1, keepdims=True) + EPS)
        norm_ref[...] = (v * scale * ag_ref[...].reshape(1, width)).astype(BF)


def convolve(x, before, after, conv_gain, conv_weight, conv_bias, attn_gain):
    rows, width = x.shape[0] // 2, x.shape[1]
    taps = conv_weight.shape[0]
    tile = 256
    out = jax.ShapeDtypeStruct((rows, width), BF)
    vector = full((width,))
    return pl.pallas_call(
        conv_kernel,
        out_shape=(out, out),
        grid=(width // tile,),
        in_specs=[full(x.shape), full((2, width)), full((2, width)), vector, vector, vector, ANYWHERE],
        out_specs=(full((rows, width)), full((rows, width))),
        scratch_shapes=[
            pltpu.VMEM((6, rows, width), BF),
            pltpu.VMEM((2, rows, width), BF),
            pltpu.VMEM((2, rows + 16, width), F32),
            pltpu.VMEM((width // 128, 128, 128), F32),
            pltpu.VMEM((width // 128, 128, 128), F32),
            pltpu.VMEM((2, taps, width, tile), BF),
            pltpu.SemaphoreType.DMA((2,)),
        ],
        compiler_params=pltpu.CompilerParams(vmem_limit_bytes=36 * MIB),
        cost_estimate=SMALL,
        name="conv",
    )(x, before, after, conv_gain, conv_bias, attn_gain, conv_weight)


def to_same_core(block):
    groups = [[i * 2 + c for i in range(8)] for c in range(2)]
    return lax.all_to_all(block, "seq", 0, 0, tiled=True, axis_index_groups=groups)


def weights_to_same_core(block):
    groups = [
        [device(x, y if i % 2 == 0 else 1 - y, i // 2, i % 2, c) for i in range(8)]
        for x in range(4)
        for y in range(2)
        for c in range(2)
    ]
    return lax.all_to_all(block, AXES, 0, 0, tiled=True, axis_index_groups=groups)


def swapped(pieces):
    return [send(p, OTHER_CORE) for p in pieces]


def own_place():
    return lax.axis_index("dp") // 2, lax.rem(lax.axis_index("seq"), 2)


def fill(mine, theirs, buf, sems):
    x, c = own_place()
    n = buf.shape[-1] // 4
    low, high = pl.ds(0, 4), pl.ds(4, 4)
    copies = []
    for core, pieces in ((c, mine), (1 - c, theirs)):
        for d, rows, src in zip((0, 3, 1, 2, 2), (pl.ds(0, 8),) * 3 + (low, high), pieces):
            cols = pl.ds(pl.multiple_of(lax.rem(x + d, 4) * n, 128), n)
            dst = buf.at[rows, core, :, cols]
            copies.append(pltpu.make_async_copy(src, dst, sems.at[len(copies)]))
    for copy in copies:
        copy.start()
    return copies


def pack_kernel(q_hbm, o_hbm, kv_hbm, out_hbm, buf, in_sems, out_sems):
    x, _ = own_place()
    copies, at = [], 0
    for src, index, n in (
        (q_hbm, 0, q_hbm.shape[1]),
        (o_hbm, x, o_hbm.shape[1] // 4),
        (kv_hbm, 0, kv_hbm.shape[1]),
    ):
        part = src if src is not o_hbm else src.at[:, pl.ds(pl.multiple_of(index * n, 128), n)]
        copies.append(
            pltpu.make_async_copy(part, buf.at[:, pl.ds(at, n)], in_sems.at[len(copies)])
        )
        at += n
    for copy in copies:
        copy.start()
    for copy in copies:
        copy.wait()
    copies = [
        pltpu.make_async_copy(buf, out_hbm.at[i], out_sems.at[i]) for i in range(out_hbm.shape[0])
    ]
    for copy in copies:
        copy.start()
    for copy in copies:
        copy.wait()


def pack(q_weight, o_weight, kv_weight):
    rows = q_weight.shape[0]
    n = q_weight.shape[1] + o_weight.shape[1] // 4 + kv_weight.shape[1]
    return pl.pallas_call(
        pack_kernel,
        out_shape=jax.ShapeDtypeStruct((8, rows, n), BF),
        in_specs=[ANYWHERE] * 3,
        out_specs=ANYWHERE,
        scratch_shapes=[
            pltpu.VMEM((rows, n), BF),
            pltpu.SemaphoreType.DMA((3,)),
            pltpu.SemaphoreType.DMA((8,)),
        ],
        compiler_params=pltpu.CompilerParams(vmem_limit_bytes=VMEM_LIMIT),
        cost_estimate=SMALL,
        name="pack",
    )(q_weight, o_weight, kv_weight)


def rotated(v, c, s):
    return v * c + pltpu.roll(v, DK // 2, 1) * s


def kv_kernel(norm_ref, cos_ref, sin_ref, own, other, kv_ref, q_ref, o_ref, buf, sems):
    _, c = own_place()
    qn, on, n = q_ref.shape[2], o_ref.shape[2], other.shape[2]
    copies = [
        pltpu.make_async_copy(own.at[:, :, pl.ds(qn + on, n)], buf.at[:, c], sems.at[0]),
        pltpu.make_async_copy(other, buf.at[:, 1 - c], sems.at[1]),
        pltpu.make_async_copy(own.at[:, :, pl.ds(0, qn)], q_ref, sems.at[2]),
        pltpu.make_async_copy(own.at[:, :, pl.ds(qn, on)], o_ref, sems.at[3]),
    ]
    for copy in copies:
        copy.start()
    for copy in copies[:2]:
        copy.wait()
    x = norm_ref[...]
    rows, width = x.shape
    kv = jnp.dot(x, buf[...].reshape(width, buf.shape[-1]), preferred_element_type=F32)
    tail = kv[:, 2 * DK :]
    packed = jnp.concatenate(
        [
            rotated(kv[:, :DK], cos_ref[...], sin_ref[...]),
            kv[:, DK : 2 * DK],
            jnp.concatenate([tail[: rows // 2], tail[rows // 2 :]], axis=1),
        ],
        axis=0,
    ).astype(BF)
    for i in range(kv_ref.shape[0]):
        kv_ref[i] = packed
    for copy in copies[2:]:
        copy.wait()


def key_values(normed, cosine, sine, own, other, qn, on):
    rows = normed.shape[0]
    return pl.pallas_call(
        kv_kernel,
        out_shape=(
            jax.ShapeDtypeStruct((8, rows * 5 // 2, DK), BF),
            jax.ShapeDtypeStruct((*own.shape[:2], qn), BF),
            jax.ShapeDtypeStruct((*own.shape[:2], on), BF),
        ),
        in_specs=[IN_VMEM, IN_VMEM, IN_VMEM, ANYWHERE, ANYWHERE],
        out_specs=(IN_VMEM, IN_VMEM, IN_VMEM),
        scratch_shapes=[
            pltpu.VMEM((8, 2, *other.shape[1:]), BF),
            pltpu.SemaphoreType.DMA((4,)),
        ],
        compiler_params=pltpu.CompilerParams(vmem_limit_bytes=48 * MIB),
        cost_estimate=SMALL,
        name="key_values",
    )(normed, cosine, sine, own, other)


def query_kernel(norm_ref, cos_ref, sin_ref, own, other, q_ref, buf, sems):
    _, core = own_place()
    copies = [
        pltpu.make_async_copy(own, buf.at[:, core], sems.at[0]),
        pltpu.make_async_copy(other, buf.at[:, 1 - core], sems.at[1]),
    ]
    for copy in copies:
        copy.start()
    for copy in copies:
        copy.wait()
    x = norm_ref[...]
    c, s = cos_ref[...], sin_ref[...]
    y = jnp.dot(x, buf[...].reshape(x.shape[1], buf.shape[-1]), preferred_element_type=F32)
    for h in range(HEADS):
        q_ref[h] = rotated(y[:, h * DK : (h + 1) * DK], c, s).astype(BF)


def queries(normed, cosine, sine, own, other):
    rows, _ = normed.shape
    return pl.pallas_call(
        query_kernel,
        out_shape=jax.ShapeDtypeStruct((HEADS, rows, DK), BF),
        in_specs=[IN_VMEM, IN_VMEM, IN_VMEM, ANYWHERE, ANYWHERE],
        scratch_shapes=[
            pltpu.VMEM((8, 2, *other.shape[1:]), BF),
            pltpu.SemaphoreType.DMA((2,)),
        ],
        compiler_params=pltpu.CompilerParams(vmem_limit_bytes=16 * MIB),
        cost_estimate=SMALL,
        name="queries",
    )(normed, cosine, sine, own, other)


def attention_kernel(
    q_ref, own, other, out_ref, kbuf, vbuf, tails, even_s, odd_s, peak, heads_s, sems
):
    heads, rows, _ = q_ref.shape
    slabs = kbuf.shape[0]
    half = rows // 2
    copies = []
    for i, part in enumerate((own, other)):
        to = pl.ds(i * (slabs // 2), slabs // 2)
        for lo, size, dst in (
            (0, rows, kbuf.at[to]),
            (rows, rows, vbuf.at[to, :, pl.ds(0, DK)]),
            (2 * rows, half, tails.at[to]),
        ):
            copies.append(
                pltpu.make_async_copy(part.at[:, pl.ds(lo, size), :], dst, sems.at[len(copies)])
            )
    for i in (0, 3, 1, 2, 4, 5):
        copies[i].start()
    copies[0].wait()
    copies[3].wait()
    chunks, _, chunk = even_s.shape
    n = chunk // rows
    scale = DK ** (-0.5) * math.log2(math.e)
    lowest = jnp.full((rows, DK), -jnp.inf, F32)

    def make_scores(head, to):
        top = lowest
        for kc in range(chunks):
            k = kbuf[kc * n : (kc + 1) * n].reshape(chunk, DK)
            s = lax.dot_general(
                q_ref[head], k, (((1,), (1,)), ((), ())), preferred_element_type=F32
            )
            to[kc] = s
            for j in range(chunk // DK):
                top = jnp.maximum(top, s[:, j * DK : (j + 1) * DK])
        return jnp.broadcast_to(jnp.max(top, axis=-1, keepdims=True), (rows, DK))

    def use_scores(head, scores, m):
        total = jnp.zeros((rows, 2 * DK), F32)
        for kc in range(chunks):
            s = scores[kc]
            w = jnp.concatenate(
                [jnp.exp2((s[:, j * DK : (j + 1) * DK] - m) * scale) for j in range(chunk // DK)],
                axis=1,
            ).astype(BF)
            v = vbuf[kc * n : (kc + 1) * n].reshape(chunk, 2 * DK)
            total = total + jnp.dot(w, v, preferred_element_type=F32)
        heads_s[head] = total[:, :DV] / total[:, DV : DV + 1]

    peak[...] = make_scores(0, even_s)
    for i in (1, 2, 4, 5):
        copies[i].wait()
    lane = lax.broadcasted_iota(jnp.int32, (half, DK), 1)
    ones = jnp.where(lane == DK // 2, 1.0, 0.0)
    for i in range(slabs):
        t = tails[i].astype(F32)
        vbuf[i, :half, DK:] = jnp.where(lane < DK // 2, t, ones).astype(BF)
        vbuf[i, half:, DK:] = jnp.where(
            lane < DK // 2, pltpu.roll(t, DK // 2, 1), ones
        ).astype(BF)

    def step(i, _):
        head = 2 * i
        m = peak[...]
        above = make_scores(head + 1, odd_s)
        use_scores(head, even_s, m)
        peak[...] = make_scores(head + 2, even_s)
        use_scores(head + 1, odd_s, above)
        return 0

    lax.fori_loop(0, heads // 2 - 1, step, 0)
    m = peak[...]
    above = make_scores(heads - 1, odd_s)
    use_scores(heads - 2, even_s, m)
    use_scores(heads - 1, odd_s, above)
    for h in range(0, heads, 2):
        out_ref[:, h * DV : (h + 2) * DV] = jnp.concatenate(
            [heads_s[h], heads_s[h + 1]], axis=1
        ).astype(BF)


def attention(q, own, other):
    heads, rows, _ = q.shape
    slabs = 2 * own.shape[0]
    tokens = slabs * rows
    chunk = 2048
    return pl.pallas_call(
        attention_kernel,
        out_shape=jax.ShapeDtypeStruct((rows, heads * DV), BF),
        in_specs=[IN_VMEM, ANYWHERE, ANYWHERE],
        scratch_shapes=[
            pltpu.VMEM((slabs, rows, DK), BF),
            pltpu.VMEM((slabs, rows, 2 * DK), BF),
            pltpu.VMEM((slabs, rows // 2, DK), BF),
            pltpu.VMEM((tokens // chunk, rows, chunk), F32),
            pltpu.VMEM((tokens // chunk, rows, chunk), F32),
            pltpu.VMEM((rows, DK), F32),
            pltpu.VMEM((heads, rows, DV), F32),
            pltpu.SemaphoreType.DMA((6,)),
        ],
        compiler_params=pltpu.CompilerParams(vmem_limit_bytes=32 * MIB),
        cost_estimate=SMALL,
        name="attention",
    )(q, own, other)


def output_kernel(mixed_ref, skip_ref, *rest):
    pieces, (out_ref, buf, sems) = rest[:10], rest[10:]
    for copy in fill(pieces[:5], pieces[5:], buf, sems):
        copy.wait()
    left = mixed_ref[...]
    y = jnp.dot(left, buf[...].reshape(left.shape[1], buf.shape[-1]), preferred_element_type=F32)
    out_ref[...] = (skip_ref[...].astype(F32) + y).astype(BF)


def output(mixed, skip, pieces):
    rows, width = skip.shape
    return pl.pallas_call(
        output_kernel,
        out_shape=jax.ShapeDtypeStruct((rows, width), BF),
        in_specs=[IN_VMEM, IN_VMEM] + [ANYWHERE] * 10,
        scratch_shapes=[
            pltpu.VMEM((8, 2, pieces[0].shape[1], width), BF),
            pltpu.SemaphoreType.DMA((10,)),
        ],
        compiler_params=pltpu.CompilerParams(vmem_limit_bytes=16 * MIB),
        cost_estimate=SMALL,
        name="output",
    )(mixed, skip, *pieces)


def rotation(seq, rows):
    half = DK // 2
    freqs = jnp.power(10000.0, -jnp.arange(half, dtype=F32) / half)
    positions = seq * rows + jnp.arange(rows, dtype=jnp.int32)
    angle = positions.astype(F32)[:, None] * freqs[None, :]
    c, s = jnp.cos(angle), jnp.sin(angle)
    return jnp.concatenate([c, c], 1), jnp.concatenate([-s, s], 1)


def tied(value, *after):
    return lax.optimization_barrier((value, *after))[0]


def halos(x, seq):
    core = seq % 2
    first, last = x[:2], x[-2:]
    ends = [(l, l + 1) for l in range(128) if l % 2 and l % 16 != 15]
    outer = send(jnp.where(core == 0, first, last), ends + [(j, i) for i, j in ends])
    inner = send(jnp.where(core == 0, last, first), OTHER_CORE)
    return jnp.where(core == 0, outer, inner), jnp.where(core == 0, inner, outer)


def body(x, conv_gain, conv_weight, conv_bias, attn_gain, q_weight, kv_weight, o_weight):
    rows = x.shape[0] // 2
    seq = lax.axis_index("seq")
    qn, on = q_weight.shape[1], o_weight.shape[1] // 4
    before, after = halos(x, seq)
    block = pack(q_weight, o_weight, kv_weight)
    block, before, after = lax.optimization_barrier((block, before, after))
    block = weights_to_same_core(block)
    skip, normed = convolve(x, before, after, conv_gain, conv_weight, conv_bias, attn_gain)
    cosine, sine = rotation(seq, rows)
    block = tied(block, normed)
    kv, q_own, o_own = key_values(
        normed, cosine, sine, block, send(block[:, :, qn + on :], OTHER_CORE), qn, on
    )
    kv_same = to_same_core(kv)
    o_left, o_right = send(o_own, along_x(1)), send(o_own, along_x(-1))
    o_parts = [o_own, o_left, o_right]
    q = queries(normed, cosine, sine, q_own, send(q_own, OTHER_CORE))
    kv_same = tied(kv_same, q, o_left, o_right)
    mixed = attention(q, kv_same, send(kv_same, OTHER_CORE))
    o_last = [send(o_left[:4], along_x(1)), send(o_right[4:], along_x(-1))]
    o_other = swapped(o_parts) + swapped([tied(p, mixed) for p in o_last])
    return skip, output(mixed, skip, o_parts + o_last + o_other)


def solution(mesh):
    rows = P(("dp", "seq"), None)
    in_specs = (rows, P(), P(), P(), P(), P("seq", None), P("seq", None), P("seq", None))
    return jax.shard_map(
        body, mesh=mesh, in_specs=in_specs, out_specs=(rows, rows), check_vma=False
    )
```

```python
import functools
import math

import jax
import jax.numpy as jnp
from jax import lax
from jax.experimental import pallas as pl
from jax.experimental.pallas import tpu as pltpu
from jax.sharding import PartitionSpec as P

HEADS = 8
DK = 128
DV = 192
EPS = 1e-06
BF = jnp.bfloat16
F32 = jnp.float32
AXES = ("dp", "seq")
MIB = 1024 * 1024
VMEM_LIMIT = 60 * MIB
SMALL = pl.CostEstimate(flops=1000, bytes_accessed=1000, transcendentals=0)


def place(l):
    dp, s = divmod(l, 16)
    return dp // 2, dp % 2, s // 4, (s // 2) % 2, s % 2


def device(x, yl, z, yh, c):
    return ((x % 4) * 2 + yl) * 16 + (z % 4) * 4 + yh * 2 + c


def moves(f):
    return [(l, device(*f(*place(l)))) for l in range(128)]


def along_x(k):
    return moves(lambda x, yl, z, yh, c: (x + k, yl, z, yh, c))


OTHER_CORE = moves(lambda x, yl, z, yh, c: (x, yl, z, yh, 1 - c))


def send(array, pairs):
    return lax.ppermute(array, AXES, pairs)


def full(shape):
    return pl.BlockSpec(shape, lambda *_: (0,) * len(shape))


ANYWHERE = pl.BlockSpec(memory_space=pl.ANY)
IN_VMEM = pl.BlockSpec(memory_space=pltpu.VMEM)


def conv_kernel(
    x_ref, before_ref, after_ref, cg_ref, bias_ref, ag_ref, w_hbm,
    skip_ref, norm_ref, lhs, raw, wide, act_s, raw_s, w_buf, sems,
):
    n = pl.program_id(0)
    steps = pl.num_programs(0)
    rows, width = skip_ref.shape
    taps, _, tile = w_buf.shape[1:]

    def weights(i):
        cols = pl.ds(pl.multiple_of(i * tile, tile), tile)
        slot = lax.rem(i, 2)
        return pltpu.make_async_copy(w_hbm.at[:, :, cols], w_buf.at[slot], sems.at[slot])

    def activated(v):
        scale = lax.rsqrt(jnp.mean(v * v, axis=-1, keepdims=True) + EPS)
        return jax.nn.gelu(v * scale * cg_ref[...].reshape(1, width), approximate=True)

    @pl.when(n == 0)
    def _():
        weights(0).start()
        groups, some, lanes = act_s.shape

        def step(i, _):
            at = pl.multiple_of(i * some, some)
            half = pl.ds(pl.multiple_of(i * (some // 2), some // 2), some // 2)
            there = pl.ds(pl.multiple_of(i * (some // 2) + 8, 8), some // 2)
            v = x_ref[pl.ds(at, some), :].astype(F32)
            g = activated(v)
            for k in range(groups):
                cols = slice(k * lanes, (k + 1) * lanes)
                raw_s[k] = v[:, cols]
                act_s[k] = g[:, cols]
                for j in range(2):
                    a = act_s[k, pl.ds(j, some // 2, 2), :]
                    wide[j, there, cols] = a
                    lhs[2 + j, half, cols] = a.astype(BF)
                    raw[j, half, cols] = raw_s[k, pl.ds(j, some // 2, 2), :].astype(BF)
            return 0

        lax.fori_loop(0, x_ref.shape[0] // some, step, 0)
        before = activated(before_ref[...].astype(F32))
        after = activated(after_ref[...].astype(F32))
        for j in range(2):
            wide[j, 7:8, :] = before[j : j + 1]
            wide[j, rows + 8 : rows + 9, :] = after[j : j + 1]
            lhs[j] = wide[j, pl.ds(7, rows), :].astype(BF)
            lhs[4 + j] = wide[j, pl.ds(9, rows), :].astype(BF)

    @pl.when(n + 1 < steps)
    def _():
        weights(n + 1).start()

    weights(n).wait()
    slot = lax.rem(n, 2)
    acc = jnp.zeros((2 * rows, tile), F32)
    for t in range(taps):
        acc = acc + jnp.dot(
            lhs[t : t + 2].reshape(2 * rows, width), w_buf[slot, t], preferred_element_type=F32
        )
    cols = pl.ds(pl.multiple_of(n * tile, tile), tile)
    bias = bias_ref[cols].reshape(1, tile)
    even = raw[0, :, cols].astype(F32) + (acc[:rows] + bias)
    odd = raw[1, :, cols].astype(F32) + (acc[rows:] + bias)
    skip_ref[:, cols] = jnp.maximum(even, odd).astype(BF)

    @pl.when(n == steps - 1)
    def _():
        v = skip_ref[...].astype(F32)
        scale = lax.rsqrt(jnp.mean(v * v, axis=-1, keepdims=True) + EPS)
        norm_ref[...] = (v * scale * ag_ref[...].reshape(1, width)).astype(BF)


def convolve(x, before, after, conv_gain, conv_weight, conv_bias, attn_gain):
    rows, width = x.shape[0] // 2, x.shape[1]
    taps = conv_weight.shape[0]
    tile = 256
    out = jax.ShapeDtypeStruct((rows, width), BF)
    vector = full((width,))
    return pl.pallas_call(
        conv_kernel,
        out_shape=(out, out),
        grid=(width // tile,),
        in_specs=[full(x.shape), full((2, width)), full((2, width)), vector, vector, vector, ANYWHERE],
        out_specs=(full((rows, width)), full((rows, width))),
        scratch_shapes=[
            pltpu.VMEM((6, rows, width), BF),
            pltpu.VMEM((2, rows, width), BF),
            pltpu.VMEM((2, rows + 16, width), F32),
            pltpu.VMEM((width // 128, 128, 128), F32),
            pltpu.VMEM((width // 128, 128, 128), F32),
            pltpu.VMEM((2, taps, width, tile), BF),
            pltpu.SemaphoreType.DMA((2,)),
        ],
        compiler_params=pltpu.CompilerParams(vmem_limit_bytes=34 * MIB),
        cost_estimate=SMALL,
        name="conv",
    )(x, before, after, conv_gain, conv_bias, attn_gain, conv_weight)


def to_same_core(block):
    groups = [[i * 2 + c for i in range(8)] for c in range(2)]
    return lax.all_to_all(block, "seq", 0, 0, tiled=True, axis_index_groups=groups)


def weights_to_same_core(block):
    groups = [
        [device(x, y if i % 2 == 0 else 1 - y, i // 2, i % 2, c) for i in range(8)]
        for x in range(4)
        for y in range(2)
        for c in range(2)
    ]
    return lax.all_to_all(block, AXES, 0, 0, tiled=True, axis_index_groups=groups)


def swapped(pieces):
    return [send(p, OTHER_CORE) for p in pieces]


def own_place():
    return lax.axis_index("dp") // 2, lax.rem(lax.axis_index("seq"), 2)


def fill(mine, theirs, buf, sems):
    x, c = own_place()
    n = buf.shape[-1] // 4
    low, high = pl.ds(0, 4), pl.ds(4, 4)
    copies = []
    for core, pieces in ((c, mine), (1 - c, theirs)):
        for d, rows, src in zip((0, 3, 1, 2, 2), (pl.ds(0, 8),) * 3 + (low, high), pieces):
            cols = pl.ds(pl.multiple_of(lax.rem(x + d, 4) * n, 128), n)
            dst = buf.at[rows, core, :, cols]
            copies.append(pltpu.make_async_copy(src, dst, sems.at[len(copies)]))
    for copy in copies:
        copy.start()
    return copies


def pack_kernel(q_hbm, o_hbm, kv_hbm, out_hbm, buf, in_sems, out_sems):
    x, _ = own_place()
    copies, at = [], 0
    for src, index, n in (
        (q_hbm, 0, q_hbm.shape[1]),
        (o_hbm, x, o_hbm.shape[1] // 4),
        (kv_hbm, 0, kv_hbm.shape[1]),
    ):
        part = src if src is not o_hbm else src.at[:, pl.ds(pl.multiple_of(index * n, 128), n)]
        copies.append(
            pltpu.make_async_copy(part, buf.at[:, pl.ds(at, n)], in_sems.at[len(copies)])
        )
        at += n
    for copy in copies:
        copy.start()
    for copy in copies:
        copy.wait()
    copies = [
        pltpu.make_async_copy(buf, out_hbm.at[i], out_sems.at[i]) for i in range(out_hbm.shape[0])
    ]
    for copy in copies:
        copy.start()
    for copy in copies:
        copy.wait()


def pack(q_weight, o_weight, kv_weight):
    rows = q_weight.shape[0]
    n = q_weight.shape[1] + o_weight.shape[1] // 4 + kv_weight.shape[1]
    return pl.pallas_call(
        pack_kernel,
        out_shape=jax.ShapeDtypeStruct((8, rows, n), BF),
        in_specs=[ANYWHERE] * 3,
        out_specs=ANYWHERE,
        scratch_shapes=[
            pltpu.VMEM((rows, n), BF),
            pltpu.SemaphoreType.DMA((3,)),
            pltpu.SemaphoreType.DMA((8,)),
        ],
        compiler_params=pltpu.CompilerParams(vmem_limit_bytes=VMEM_LIMIT),
        cost_estimate=SMALL,
        name="pack",
    )(q_weight, o_weight, kv_weight)


def rotated(v, c, s):
    return v * c + pltpu.roll(v, DK // 2, 1) * s


def kv_kernel(norm_ref, cos_ref, sin_ref, own, other, kv_ref, q_ref, o_ref, buf, sems):
    _, c = own_place()
    qn, on, n = q_ref.shape[2], o_ref.shape[2], other.shape[2]
    copies = [
        pltpu.make_async_copy(own.at[:, :, pl.ds(qn + on, n)], buf.at[:, c], sems.at[0]),
        pltpu.make_async_copy(other, buf.at[:, 1 - c], sems.at[1]),
        pltpu.make_async_copy(own.at[:, :, pl.ds(0, qn)], q_ref, sems.at[2]),
        pltpu.make_async_copy(own.at[:, :, pl.ds(qn, on)], o_ref, sems.at[3]),
    ]
    for copy in copies:
        copy.start()
    for copy in copies[:2]:
        copy.wait()
    x = norm_ref[...]
    rows, width = x.shape
    kv = jnp.dot(x, buf[...].reshape(width, buf.shape[-1]), preferred_element_type=F32)
    tail = kv[:, 2 * DK :]
    packed = jnp.concatenate(
        [
            rotated(kv[:, :DK], cos_ref[...], sin_ref[...]),
            kv[:, DK : 2 * DK],
            jnp.concatenate([tail[: rows // 2], tail[rows // 2 :]], axis=1),
        ],
        axis=0,
    ).astype(BF)
    for i in range(kv_ref.shape[0]):
        kv_ref[i] = packed
    for copy in copies[2:]:
        copy.wait()


def key_values(normed, cosine, sine, own, other, qn, on):
    rows = normed.shape[0]
    return pl.pallas_call(
        kv_kernel,
        out_shape=(
            jax.ShapeDtypeStruct((8, rows * 5 // 2, DK), BF),
            jax.ShapeDtypeStruct((*own.shape[:2], qn), BF),
            jax.ShapeDtypeStruct((*own.shape[:2], on), BF),
        ),
        in_specs=[IN_VMEM, IN_VMEM, IN_VMEM, ANYWHERE, ANYWHERE],
        out_specs=(IN_VMEM, IN_VMEM, IN_VMEM),
        scratch_shapes=[
            pltpu.VMEM((8, 2, *other.shape[1:]), BF),
            pltpu.SemaphoreType.DMA((4,)),
        ],
        compiler_params=pltpu.CompilerParams(vmem_limit_bytes=48 * MIB),
        cost_estimate=SMALL,
        name="key_values",
    )(normed, cosine, sine, own, other)


def query_kernel(norm_ref, cos_ref, sin_ref, own, other, q_ref, buf, sems):
    _, core = own_place()
    copies = [
        pltpu.make_async_copy(own, buf.at[:, core], sems.at[0]),
        pltpu.make_async_copy(other, buf.at[:, 1 - core], sems.at[1]),
    ]
    for copy in copies:
        copy.start()
    for copy in copies:
        copy.wait()
    x = norm_ref[...]
    c, s = cos_ref[...], sin_ref[...]
    y = jnp.dot(x, buf[...].reshape(x.shape[1], buf.shape[-1]), preferred_element_type=F32)
    for h in range(HEADS):
        q_ref[h] = rotated(y[:, h * DK : (h + 1) * DK], c, s).astype(BF)


def queries(normed, cosine, sine, own, other):
    rows, _ = normed.shape
    return pl.pallas_call(
        query_kernel,
        out_shape=jax.ShapeDtypeStruct((HEADS, rows, DK), BF),
        in_specs=[IN_VMEM, IN_VMEM, IN_VMEM, ANYWHERE, ANYWHERE],
        scratch_shapes=[
            pltpu.VMEM((8, 2, *other.shape[1:]), BF),
            pltpu.SemaphoreType.DMA((2,)),
        ],
        compiler_params=pltpu.CompilerParams(vmem_limit_bytes=16 * MIB),
        cost_estimate=SMALL,
        name="queries",
    )(normed, cosine, sine, own, other)


def attention_kernel(
    q_ref, own, other, out_ref, kbuf, vbuf, tails, even_s, odd_s, peak, heads_s, sems
):
    heads, rows, _ = q_ref.shape
    slabs = kbuf.shape[0]
    half = rows // 2
    copies = []
    for i, part in enumerate((own, other)):
        to = pl.ds(i * (slabs // 2), slabs // 2)
        for lo, size, dst in (
            (0, rows, kbuf.at[to]),
            (rows, rows, vbuf.at[to, :, pl.ds(0, DK)]),
            (2 * rows, half, tails.at[to]),
        ):
            copies.append(
                pltpu.make_async_copy(part.at[:, pl.ds(lo, size), :], dst, sems.at[len(copies)])
            )
    for i in (0, 3, 1, 2, 4, 5):
        copies[i].start()
    copies[0].wait()
    copies[3].wait()
    chunks, _, chunk = even_s.shape
    n = chunk // rows
    scale = DK ** (-0.5) * math.log2(math.e)
    lowest = jnp.full((rows, DK), -jnp.inf, F32)

    def make_scores(head, to):
        top = lowest
        for kc in range(chunks):
            k = kbuf[kc * n : (kc + 1) * n].reshape(chunk, DK)
            s = lax.dot_general(
                q_ref[head], k, (((1,), (1,)), ((), ())), preferred_element_type=F32
            )
            to[kc] = s
            for j in range(chunk // DK):
                top = jnp.maximum(top, s[:, j * DK : (j + 1) * DK])
        return jnp.broadcast_to(jnp.max(top, axis=-1, keepdims=True), (rows, DK))

    def use_scores(head, scores, m):
        total = jnp.zeros((rows, 2 * DK), F32)
        for kc in range(chunks):
            s = scores[kc]
            w = jnp.concatenate(
                [jnp.exp2((s[:, j * DK : (j + 1) * DK] - m) * scale) for j in range(chunk // DK)],
                axis=1,
            ).astype(BF)
            v = vbuf[kc * n : (kc + 1) * n].reshape(chunk, 2 * DK)
            total = total + jnp.dot(w, v, preferred_element_type=F32)
        heads_s[head] = total[:, :DV] / total[:, DV : DV + 1]

    peak[...] = make_scores(0, even_s)
    for i in (1, 2, 4, 5):
        copies[i].wait()
    lane = lax.broadcasted_iota(jnp.int32, (half, DK), 1)
    ones = jnp.where(lane == DK // 2, 1.0, 0.0)
    for i in range(slabs):
        t = tails[i].astype(F32)
        vbuf[i, :half, DK:] = jnp.where(lane < DK // 2, t, ones).astype(BF)
        vbuf[i, half:, DK:] = jnp.where(
            lane < DK // 2, pltpu.roll(t, DK // 2, 1), ones
        ).astype(BF)

    def step(i, _):
        head = 2 * i
        m = peak[...]
        above = make_scores(head + 1, odd_s)
        use_scores(head, even_s, m)
        peak[...] = make_scores(head + 2, even_s)
        use_scores(head + 1, odd_s, above)
        return 0

    lax.fori_loop(0, heads // 2 - 1, step, 0)
    m = peak[...]
    above = make_scores(heads - 1, odd_s)
    use_scores(heads - 2, even_s, m)
    use_scores(heads - 1, odd_s, above)
    for h in range(0, heads, 2):
        out_ref[:, h * DV : (h + 2) * DV] = jnp.concatenate(
            [heads_s[h], heads_s[h + 1]], axis=1
        ).astype(BF)


def attention(q, own, other):
    heads, rows, _ = q.shape
    slabs = 2 * own.shape[0]
    tokens = slabs * rows
    chunk = 2048
    return pl.pallas_call(
        attention_kernel,
        out_shape=jax.ShapeDtypeStruct((rows, heads * DV), BF),
        in_specs=[IN_VMEM, ANYWHERE, ANYWHERE],
        scratch_shapes=[
            pltpu.VMEM((slabs, rows, DK), BF),
            pltpu.VMEM((slabs, rows, 2 * DK), BF),
            pltpu.VMEM((slabs, rows // 2, DK), BF),
            pltpu.VMEM((tokens // chunk, rows, chunk), F32),
            pltpu.VMEM((tokens // chunk, rows, chunk), F32),
            pltpu.VMEM((rows, DK), F32),
            pltpu.VMEM((heads, rows, DV), F32),
            pltpu.SemaphoreType.DMA((6,)),
        ],
        compiler_params=pltpu.CompilerParams(vmem_limit_bytes=24 * MIB),
        cost_estimate=SMALL,
        name="attention",
    )(q, own, other)


def output_kernel(mixed_ref, skip_ref, *rest):
    pieces, (out_ref, buf, sems) = rest[:10], rest[10:]
    for copy in fill(pieces[:5], pieces[5:], buf, sems):
        copy.wait()
    left = mixed_ref[...]
    y = jnp.dot(left, buf[...].reshape(left.shape[1], buf.shape[-1]), preferred_element_type=F32)
    out_ref[...] = (skip_ref[...].astype(F32) + y).astype(BF)


def output(mixed, skip, pieces):
    rows, width = skip.shape
    return pl.pallas_call(
        output_kernel,
        out_shape=jax.ShapeDtypeStruct((rows, width), BF),
        in_specs=[IN_VMEM, IN_VMEM] + [ANYWHERE] * 10,
        scratch_shapes=[
            pltpu.VMEM((8, 2, pieces[0].shape[1], width), BF),
            pltpu.SemaphoreType.DMA((10,)),
        ],
        compiler_params=pltpu.CompilerParams(vmem_limit_bytes=16 * MIB),
        cost_estimate=SMALL,
        name="output",
    )(mixed, skip, *pieces)


def rotation(seq, rows):
    half = DK // 2
    freqs = jnp.power(10000.0, -jnp.arange(half, dtype=F32) / half)
    positions = seq * rows + jnp.arange(rows, dtype=jnp.int32)
    angle = positions.astype(F32)[:, None] * freqs[None, :]
    c, s = jnp.cos(angle), jnp.sin(angle)
    return jnp.concatenate([c, c], 1), jnp.concatenate([-s, s], 1)


def tied(value, *after):
    return lax.optimization_barrier((value, *after))[0]


def halos(x, seq):
    core = seq % 2
    first, last = x[:2], x[-2:]
    ends = [(l, l + 1) for l in range(128) if l % 2 and l % 16 != 15]
    outer = send(jnp.where(core == 0, first, last), ends + [(j, i) for i, j in ends])
    inner = send(jnp.where(core == 0, last, first), OTHER_CORE)
    return jnp.where(core == 0, outer, inner), jnp.where(core == 0, inner, outer)


def body(x, conv_gain, conv_weight, conv_bias, attn_gain, q_weight, kv_weight, o_weight):
    rows = x.shape[0] // 2
    seq = lax.axis_index("seq")
    qn, on = q_weight.shape[1], o_weight.shape[1] // 4
    before, after = halos(x, seq)
    block = pack(q_weight, o_weight, kv_weight)
    block, before, after = lax.optimization_barrier((block, before, after))
    block = weights_to_same_core(block)
    skip, normed = convolve(x, before, after, conv_gain, conv_weight, conv_bias, attn_gain)
    cosine, sine = rotation(seq, rows)
    block = tied(block, normed)
    kv, q_own, o_own = key_values(
        normed, cosine, sine, block, send(block[:, :, qn + on :], OTHER_CORE), qn, on
    )
    kv_same = to_same_core(kv)
    o_left, o_right = send(o_own, along_x(1)), send(o_own, along_x(-1))
    o_parts = [o_own, o_left, o_right]
    q = queries(normed, cosine, sine, q_own, send(q_own, OTHER_CORE))
    kv_same = tied(kv_same, q, o_left, o_right)
    mixed = attention(q, kv_same, send(kv_same, OTHER_CORE))
    o_last = [send(o_left[:4], along_x(1)), send(o_right[4:], along_x(-1))]
    o_other = swapped(o_parts) + swapped([tied(p, mixed) for p in o_last])
    return skip, output(mixed, skip, o_parts + o_last + o_other)


def solution(mesh):
    rows = P(("dp", "seq"), None)
    in_specs = (rows, P(), P(), P(), P(), P("seq", None), P("seq", None), P("seq", None))
    return jax.shard_map(
        body, mesh=mesh, in_specs=in_specs, out_specs=(rows, rows), check_vma=False
    )
```
